32 devices in a mesh: seq: 4 (over x, core), tp: 8 (over z, y).
Axes of the slice: x: 2, y: 2, z: 4, core: 2. Of those that a mesh axis runs over, the one named last changes fastest.
Arguments:
- clean_in: bfloat16 [4, 1024, 5120], P(None, 'seq', 'tp'), may hold values from -6 to 6
- noise_mask: int32 [4, 1024], P(None, 'seq'), may hold values from 0 to 1
- mask_embed: bfloat16 [5120], P('tp'), may hold values from -6 to 6
- norm_gain: float32 [5120], replicated, may hold values from 0.1 to 1.9
- q_weight: bfloat16 [5120, 4096], P(None, 'tp'), may hold values from -0.078125 to 0.078125
- q_bias: float32 [4096], P('tp'), may hold values from -60 to 60
- k_weight: bfloat16 [5120, 1024], replicated, may hold values from -0.078125 to 0.078125
- v_weight: bfloat16 [5120, 1024], replicated, may hold values from -0.078125 to 0.078125
- v_bias: float32 [1024], replicated, may hold values from -3 to 3
- o_weight: bfloat16 [4096, 5120], P('tp'), may hold values from -0.125 to 0.125
Outputs:
- clean_out: bfloat16 [4, 1024, 5120], P(None, 'seq', 'tp')
- noisy_out: bfloat16 [4, 1024, 5120], P(None, 'seq', 'tp')
The draws below stay inside these ranges and needn't reach their ends.
All inputs are finite; a program needn't handle non-finite values.
Results may differ from the reference program's by a relative error of at most 0.013.
The reference program's roundings to bfloat16 on the way count: a program that leaves them out, or rounds other values in their place, can miss the bound.
Values may be sent and summed in bfloat16 or wider, within the bound.
A program may use at most 192 MiB of HBM per device.

```python
import math
import jax
import jax.numpy as jnp
from jax import lax

D = 5120
HD = 128
KVH = 8
QH = 32
BLOCK = 32
SEQS = 4
LENGTH = 1024


def draw_noise_mask(key, part):
    key = jax.random.fold_in(key, 11)
    rate_key, ticket_key = jax.random.split(key)
    block_count = LENGTH // BLOCK
    rates = jax.random.randint(rate_key, (SEQS, block_count, 1), 1, BLOCK + 1)
    tickets = jax.random.randint(ticket_key, (SEQS, block_count, BLOCK), 0, BLOCK)
    return (tickets < rates).astype(jnp.int32).reshape(SEQS, LENGTH)


def draw_q_bias(key, part):
    key = jax.random.fold_in(key, 23)
    base_key = jax.random.fold_in(key, 0)
    base = jax.random.normal(base_key, (QH, HD), jnp.float32)
    values = jnp.clip(base * 0.5, -3.0, 3.0)
    return values.reshape(QH * HD)


def spiked(drawn, own_key, source, target, parts, factor):
    def block_of(axis_at):
        return (jnp.arange(drawn.shape[axis_at]) // (drawn.shape[axis_at] // parts)).reshape((-1,) + (1,) * (drawn.ndim - 1 - axis_at))

    one_side = jax.random.permutation(own_key, parts)[block_of(target)]
    other_side = (block_of(target) + parts // 2) % parts
    return jnp.where((block_of(source) == one_side) | (block_of(source) == other_side), factor * drawn, drawn)


def block_levels(own_key, extent, pieces, smallest, largest):
    factor_of = 1.0
    for position, shards_of in pieces:
        heights = jax.random.uniform(jax.random.fold_in(jax.random.fold_in(own_key, 6), position), (shards_of,), jnp.float32, smallest / len(pieces), largest / len(pieces))
        factor_of = factor_of * jnp.repeat(jnp.exp(heights), extent[position] // shards_of).reshape((-1,) + (1,) * (len(extent) - 1 - position))
    return factor_of


def normal_values(stream_key, extent, width, limit, cuts=(), held_as=jnp.bfloat16):
    entries = width * jax.random.normal(stream_key, extent, jnp.float32)
    if cuts:
        entries = entries * block_levels(stream_key, extent, cuts, -0.22, 0.18)
    return jnp.clip(entries, -limit, limit).astype(held_as)


def bell_draw_with(stream_key, shape, deviation, reach, cuts, heavy, kind=jnp.bfloat16):
    drawn = deviation * jax.random.normal(stream_key, shape, jnp.float32)
    if cuts:
        drawn = drawn * block_levels(stream_key, shape, cuts, -0.22, 0.18)
    return jnp.clip(spiked(drawn, jax.random.fold_in(stream_key, 3), *heavy), -reach, reach).astype(kind)


def setup_inputs(seed: int = 0) -> dict:
    seeds = jax.random.split(jax.random.key(seed), 11)
    clean_in = normal_values(seeds[0], (SEQS, LENGTH, D), 1.0, 6.0, ((1, 4), (2, 8)))
    noise_mask = draw_noise_mask(jax.random.fold_in(seeds[10], 71), 0)
    mask_embed = normal_values(seeds[2], (D,), 1.0, 6.0, ((0, 8),))
    norm_gain = jnp.clip(1.0 + 0.18 * jax.random.normal(seeds[3], (D,), jnp.float32), 0.1, 1.9)
    q_weight = normal_values(seeds[4], (D, QH * HD), D ** -0.5, 0.078125, ((1, 8),))
    q_bias = draw_q_bias(jax.random.fold_in(seeds[10], 71), 0)
    k_weight = normal_values(seeds[6], (D, KVH * HD), D ** -0.5, 0.078125)
    v_weight = normal_values(seeds[7], (D, KVH * HD), D ** -0.5, 0.078125)
    v_bias = normal_values(seeds[8], (KVH * HD,), 0.5, 3.0, (), jnp.float32)
    o_weight = bell_draw_with(seeds[9], (QH * HD, D), (QH * HD) ** -0.5, 0.125, ((0, 8),), (0, 1, 8, 2.0))
    return dict(clean_in=clean_in, noise_mask=noise_mask, mask_embed=mask_embed, norm_gain=norm_gain, q_weight=q_weight, q_bias=q_bias, k_weight=k_weight, v_weight=v_weight, v_bias=v_bias, o_weight=o_weight)


eps = 1e-06
theta = 1000000.0

def rotate(values, positions):
    half = values.shape[-1] // 2
    freqs = theta ** (-(jnp.arange(half).astype(jnp.float32) * 2.0) / values.shape[-1])
    angles = positions[:, None] * freqs[None, :]
    cosine = jnp.cos(angles)[:, None, :]
    sine = jnp.sin(angles)[:, None, :]
    first = values[..., :half]
    second = values[..., half:]
    return jnp.concatenate([first * cosine - second * sine, second * cosine + first * sine], axis=-1)

def attend(queries, key_rows, value_rows, allowed):
    scores = jnp.einsum('qhd,khd->hqk', queries.astype(jnp.float32), key_rows.astype(jnp.float32)) * (1.0 / math.sqrt(HD))
    scores = jnp.where(allowed[None], scores, -1e+30)
    best = lax.optimization_barrier(jnp.max(scores, axis=-1, keepdims=True))
    expo = jnp.where(allowed[None], jnp.exp(scores - best), 0.0)
    denom = lax.optimization_barrier(jnp.sum(expo, axis=-1))
    weights = lax.optimization_barrier(expo.astype(jnp.bfloat16)).astype(jnp.float32)
    weighted = jnp.einsum('hqk,khd->qhd', weights, value_rows.astype(jnp.float32))
    return weighted / jnp.transpose(denom)[:, :, None]

def reference(clean_in, noise_mask, mask_embed, norm_gain, q_weight, q_bias, k_weight, v_weight, v_bias, o_weight):
    noisy_in = jnp.where(noise_mask[..., None] == 1, mask_embed[None, None, :], clean_in)
    group = QH // KVH
    positions = jnp.arange(LENGTH).astype(jnp.float32)
    blocks = jnp.arange(LENGTH) // BLOCK
    clean_seen = blocks[None, :] <= blocks[:, None]
    noisy_seen = jnp.concatenate([blocks[None, :] < blocks[:, None], blocks[None, :] == blocks[:, None]], axis=1)

    def one_doc(pair):
        streams = jnp.stack([pair[0], pair[1]])
        floats = streams.astype(jnp.float32)
        mean_sq = lax.optimization_barrier(jnp.mean(floats * floats, axis=-1, keepdims=True))
        normed = (floats * lax.rsqrt(mean_sq + eps) * norm_gain).astype(jnp.bfloat16)
        flat_rows = normed.reshape(2 * LENGTH, D)
        queries = jnp.dot(flat_rows, q_weight, preferred_element_type=jnp.float32) + q_bias
        key_rows = jnp.dot(flat_rows, k_weight, preferred_element_type=jnp.float32)
        value_rows = jnp.dot(flat_rows, v_weight, preferred_element_type=jnp.float32) + v_bias
        queries = rotate(queries.reshape(2, LENGTH, QH, HD), positions).astype(jnp.bfloat16)
        key_rows = rotate(key_rows.reshape(2, LENGTH, KVH, HD), positions).astype(jnp.bfloat16)
        value_rows = value_rows.reshape(2, LENGTH, KVH, HD).astype(jnp.bfloat16)
        key_rows = jnp.repeat(key_rows, group, axis=2)
        value_rows = jnp.repeat(value_rows, group, axis=2)
        clean_att = attend(queries[0], key_rows[0], value_rows[0], clean_seen)
        noisy_att = attend(queries[1], jnp.concatenate([key_rows[0], key_rows[1]], axis=0), jnp.concatenate([value_rows[0], value_rows[1]], axis=0), noisy_seen)
        attended = jnp.stack([clean_att, noisy_att]).astype(jnp.bfloat16).reshape(2 * LENGTH, QH * HD)
        mixed = jnp.dot(attended, o_weight, preferred_element_type=jnp.float32).reshape(2, LENGTH, D)
        return (floats + mixed).astype(jnp.bfloat16)
    outputs = lax.map(one_doc, (clean_in, noisy_in))
    return (outputs[:, 0], outputs[:, 1])
```

```python
import functools
import math

import jax
import jax.numpy as jnp
from jax import lax
from jax.experimental import pallas as pl
from jax.experimental.pallas import tpu as pltpu
from jax.sharding import PartitionSpec as P

HD = 128
KVH = 8
BLOCK = 32
PAD = 16

eps = 1e-06
theta = 1000000.0
MESH = pl.DeviceIdType.MESH
VMEM_BYTES = 56 * 2**20


def tables(positions):
    half = HD // 2
    freqs = theta ** (-(jnp.arange(half).astype(jnp.float32) * 2.0) / HD)
    angles = positions[:, None] * freqs[None, :]
    cosine = jnp.cos(angles)
    sine = jnp.sin(angles)
    return jnp.concatenate([cosine, cosine], 1), jnp.concatenate([-sine, sine], 1)


def greet(groups):
    barrier = pltpu.get_barrier_semaphore()
    count = 0
    for axis, size in groups:
        me = lax.axis_index(axis)
        for step in range(1, size):
            pl.semaphore_signal(
                barrier, inc=1, device_id={axis: lax.rem(me + step, size)}, device_id_type=MESH
            )
        count += size - 1
    pl.semaphore_wait(barrier, count)


class Gather:
    def __init__(self, axis, lines, cross, own, out, send, recv, keep):
        self.axis, self.lines, self.cross = axis, lines, cross
        self.own, self.out, self.send, self.recv = own, out, send, recv
        me = lax.axis_index(axis)
        self.me, self.a, self.b = me, me // cross, lax.rem(me, cross)
        self.local = pltpu.make_async_copy(own, out.at[me], keep)
        self.started = []

    def copy(self, slot, way, device, src):
        return pltpu.make_async_remote_copy(
            src_ref=src,
            dst_ref=self.out.at[slot],
            send_sem=self.send.at[slot, way],
            recv_sem=self.recv.at[slot],
            device_id={self.axis: device},
            device_id_type=MESH,
        )

    def pass_on(self, slot, way, here, src=None):
        step = (self.cross, -self.cross, 1, -1)[way]
        inside = (
            self.a + 1 < self.lines, self.a > 0, self.b + 1 < self.cross, self.b > 0
        )[way]
        cond = inside if here is None else jnp.logical_and(here, inside)
        source = self.out.at[slot] if src is None else src

        @pl.when(cond)
        def _():
            self.copy(slot, way, self.me + step, source).start()

        self.started.append((slot, way, step, source, cond))

    def arrived(self, slot):
        self.copy(slot, 0, lax.rem(self.me + 1, self.lines * self.cross), self.out.at[slot]).wait_recv()

    def begin(self):
        for way in range(4):
            self.pass_on(self.me, way, None, self.own)
        self.local.start()

    def along(self, r):
        for sign in (-1, 1):
            src_a = self.a + sign * r
            here = src_a >= 0 if sign < 0 else src_a < self.lines
            slot = src_a * self.cross + self.b

            @pl.when(here)
            def _():
                self.arrived(slot)

            self.pass_on(slot, 0 if sign < 0 else 1, here)
            for way in (2, 3):
                self.pass_on(slot, way, here)

    def across(self):
        for r in range(1, self.cross):
            for sign in (-1, 1):
                src_b = self.b + sign * r
                here = src_b >= 0 if sign < 0 else src_b < self.cross
                for line in range(self.lines):
                    slot = line * self.cross + src_b

                    @pl.when(here)
                    def _():
                        self.arrived(slot)

                    if self.cross > 2:
                        self.pass_on(slot, 2 if sign < 0 else 3, here)

    def finish(self):
        for slot, way, step, source, cond in self.started:

            @pl.when(cond)
            def _():
                self.copy(slot, way, self.me + step, source).wait_send()

        self.local.wait()


def gather_kernel(axis, lines, cross, own, out, send, recv, keep):
    greet([(axis, lines * cross)])
    g = Gather(axis, lines, cross, own, out, send, recv, keep)
    g.begin()
    for r in range(1, lines):
        g.along(r)
    g.across()
    g.finish()


def gather(own, axis, lines, cross, collective_id):
    n = lines * cross
    return pl.pallas_call(
        functools.partial(gather_kernel, axis, lines, cross),
        out_shape=jax.ShapeDtypeStruct((n,) + own.shape, own.dtype),
        in_specs=[pl.BlockSpec(memory_space=pl.ANY)],
        out_specs=pl.BlockSpec(memory_space=pl.ANY),
        scratch_shapes=[
            pltpu.SemaphoreType.DMA((n, 4)),
            pltpu.SemaphoreType.DMA((n,)),
            pltpu.SemaphoreType.DMA,
        ],
        compiler_params=pltpu.CompilerParams(collective_id=collective_id, has_side_effects=True),
    )(own)


def first_kernel(
    tp, seq, lines, cross, own, weight, out, wout, send, recv, keep, wsend, wrecv, wkeep, xsend, xrecv
):
    greet([("tp", tp), ("seq", seq)])
    g = Gather("tp", lines, cross, own, out, send, recv, keep)
    g.begin()
    me = lax.axis_index("tp")
    s = lax.axis_index("seq")
    rows = weight.shape[1] // seq
    piece = pl.ds(pl.multiple_of(s * rows, rows), rows)

    def deal(d):
        to = lax.rem(me + d, tp)
        return pltpu.make_async_remote_copy(
            src_ref=weight.at[to, piece],
            dst_ref=wout.at[me, piece],
            send_sem=wsend.at[d],
            recv_sem=wrecv.at[d],
            device_id={"tp": to},
            device_id_type=MESH,
        )

    def share(d, e):
        source = lax.rem(me + tp - d, tp)
        return pltpu.make_async_remote_copy(
            src_ref=wout.at[source, piece],
            dst_ref=wout.at[source, piece],
            send_sem=xsend.at[d, e],
            recv_sem=xrecv.at[d, e],
            device_id={"seq": lax.rem(s + e, seq)},
            device_id_type=MESH,
        )

    own_weight = pltpu.make_async_copy(weight.at[me], wout.at[me], wkeep)
    own_weight.start()
    for d in range(1, tp):
        deal(d).start()
    g.along(1)
    for d in range(1, tp):
        deal(d).wait_recv()
        for e in range(1, seq):
            share(d, e).start()
    for r in range(2, lines):
        g.along(r)
    g.across()
    for d in range(1, tp):
        deal(d).wait_send()
        for e in range(1, seq):
            share(d, e).wait()
    own_weight.wait()
    g.finish()


def first_gather(own, weight, tp, seq, lines, cross):
    return pl.pallas_call(
        functools.partial(first_kernel, tp, seq, lines, cross),
        out_shape=(
            jax.ShapeDtypeStruct((tp,) + own.shape, own.dtype),
            jax.ShapeDtypeStruct(weight.shape, weight.dtype),
        ),
        in_specs=[pl.BlockSpec(memory_space=pl.ANY)] * 2,
        out_specs=(pl.BlockSpec(memory_space=pl.ANY),) * 2,
        scratch_shapes=[
            pltpu.SemaphoreType.DMA((tp, 4)),
            pltpu.SemaphoreType.DMA((tp,)),
            pltpu.SemaphoreType.DMA,
            pltpu.SemaphoreType.DMA((tp,)),
            pltpu.SemaphoreType.DMA((tp,)),
            pltpu.SemaphoreType.DMA,
            pltpu.SemaphoreType.DMA((tp, seq)),
            pltpu.SemaphoreType.DMA((tp, seq)),
        ],
        compiler_params=pltpu.CompilerParams(collective_id=0, has_side_effects=True),
    )(own, weight)


def spin(values, cosine, sine):
    parts = []
    for start in range(0, values.shape[1], HD):
        head = values[:, start : start + HD]
        parts.append(head * cosine + pltpu.roll(head, HD // 2, 1) * sine)
    return jnp.concatenate(parts, 1) if len(parts) > 1 else parts[0]


def project_kernel(
    tp, head_ref, x_ref, m_ref, mask_ref, gain_ref, qw, qb, kw, vw, vb, cos_ref, sin_ref,
    q_out, kvc_out, kvn_out, qm, km, vm,
):
    del head_ref
    width = x_ref.shape[2]
    q_cols = qw.shape[1]

    def project(ref):
        rows = ref.shape[1]
        total = jnp.zeros((rows, 1), jnp.float32)
        for t in range(tp):
            part = ref[t].astype(jnp.float32)
            total = total + jnp.sum(part * part, axis=1, keepdims=True)
        scale = lax.rsqrt(total / (tp * width) + eps)
        q = jnp.zeros((rows, q_cols), jnp.float32)
        k = jnp.zeros((rows, HD), jnp.float32)
        v = jnp.zeros((rows, HD), jnp.float32)
        for t in range(tp):
            here = pl.ds(t * width, width)
            normed = (ref[t].astype(jnp.float32) * scale * gain_ref[t]).astype(jnp.bfloat16)
            q = q + jnp.dot(normed, qw[here, :], preferred_element_type=jnp.float32)
            k = k + jnp.dot(normed, kw[here, :], preferred_element_type=jnp.float32)
            v = v + jnp.dot(normed, vw[here, :], preferred_element_type=jnp.float32)
        return q + qb[...], k, v + vb[0]

    @pl.when(pl.program_id(0) == 0)
    def _():
        qm[...], km[...], vm[...] = project(m_ref)

    cosine, sine = cos_ref[...], sin_ref[...]
    rows = x_ref.shape[1]
    q, k, v = project(x_ref)
    q = spin(q, cosine, sine)
    k = spin(k, cosine, sine)
    masked = mask_ref[...] == 1
    q_mask = spin(jnp.broadcast_to(qm[0:1, :], (rows, q_cols)), cosine, sine)
    k_mask = spin(jnp.broadcast_to(km[0:1, :], (rows, HD)), cosine, sine)
    v_mask = jnp.broadcast_to(vm[0:1, :], (rows, HD))
    q_out[0] = q.astype(jnp.bfloat16)
    q_out[1] = jnp.where(masked, q_mask, q).astype(jnp.bfloat16)
    kvc_out[0] = k.astype(jnp.bfloat16)
    kvc_out[1] = v.astype(jnp.bfloat16)
    kvn_out[0] = jnp.where(masked, k_mask, k).astype(jnp.bfloat16)
    kvn_out[1] = jnp.where(masked, v_mask, v).astype(jnp.bfloat16)


def project(head, whole, mask_col, gain, q_weight, q_bias, k_weight, v_weight, v_bias, cosine, sine):
    tp, padded, width = whole.shape
    tokens = cosine.shape[0]
    rows = padded - PAD
    d_model, q_cols = q_weight.shape
    fixed = lambda *shape: pl.BlockSpec(shape, lambda i, h: (0,) * len(shape))
    return pl.pallas_call(
        functools.partial(project_kernel, tp),
        out_shape=(
            jax.ShapeDtypeStruct((2, rows, q_cols), jnp.bfloat16),
            jax.ShapeDtypeStruct((2, rows, HD), jnp.bfloat16),
            jax.ShapeDtypeStruct((2, rows, HD), jnp.bfloat16),
        ),
        grid_spec=pltpu.PrefetchScalarGridSpec(
            num_scalar_prefetch=1,
            grid=(rows // tokens,),
            in_specs=[
                pl.BlockSpec((tp, tokens, width), lambda i, h: (0, i, 0)),
                pl.BlockSpec((tp, PAD, width), lambda i, h: (0, rows // PAD, 0)),
                pl.BlockSpec((tokens, 1), lambda i, h: (i, 0)),
                fixed(tp, 1, width),
                fixed(d_model, q_cols),
                fixed(1, q_cols),
                pl.BlockSpec((d_model, HD), lambda i, h: (0, h[0])),
                pl.BlockSpec((d_model, HD), lambda i, h: (0, h[0])),
                pl.BlockSpec((1, 1, HD), lambda i, h: (h[0], 0, 0)),
                fixed(tokens, HD),
                fixed(tokens, HD),
            ],
            out_specs=(
                pl.BlockSpec((2, tokens, q_cols), lambda i, h: (0, i, 0)),
                pl.BlockSpec((2, tokens, HD), lambda i, h: (0, i, 0)),
                pl.BlockSpec((2, tokens, HD), lambda i, h: (0, i, 0)),
            ),
            scratch_shapes=[
                pltpu.VMEM((PAD, q_cols), jnp.float32),
                pltpu.VMEM((PAD, HD), jnp.float32),
                pltpu.VMEM((PAD, HD), jnp.float32),
            ],
        ),
        compiler_params=pltpu.CompilerParams(vmem_limit_bytes=VMEM_BYTES),
    )(
        head, whole, whole, mask_col, gain.reshape(tp, 1, width), q_weight, q_bias.reshape(1, -1),
        k_weight, v_weight, v_bias.reshape(-1, 1, HD), cosine, sine,
    )


def attend_kernel(seq_ref, q_ref, kv_ref, kvn_ref, out_ref):
    seq, _, tokens, _ = kv_ref.shape
    heads = q_ref.shape[2] // HD
    keys = seq * tokens
    k_all = kv_ref[:, 0].reshape(keys, HD)
    v_all = kv_ref[:, 1].reshape(keys, HD)
    k_own, v_own = kvn_ref[0], kvn_ref[1]
    scale = 1.0 / math.sqrt(HD)

    def blocks(count, axis, start):
        return (start + lax.broadcasted_iota(jnp.int32, (tokens, count), axis)) // BLOCK

    q_block = blocks(keys, 0, seq_ref[0] * tokens)
    k_block = blocks(keys, 1, 0)
    clean_bias = jnp.where(k_block <= q_block, 0.0, -1e30)
    noisy_bias = jnp.where(k_block < q_block, 0.0, -1e30)
    own_bias = jnp.where(blocks(tokens, 1, 0) == blocks(tokens, 0, 0), 0.0, -1e30)

    def scores(q, k, bias):
        dims = (((1,), (1,)), ((), ()))
        return lax.dot_general(q, k, dims, preferred_element_type=jnp.float32) * scale + bias

    def weigh(expo, v):
        return jnp.dot(expo.astype(jnp.bfloat16), v, preferred_element_type=jnp.float32)

    for h in range(heads):
        cols = pl.ds(h * HD, HD)
        s = scores(q_ref[0, :, cols], k_all, clean_bias)
        expo = jnp.exp(s - jnp.max(s, axis=1, keepdims=True))
        denom = jnp.sum(expo, axis=1, keepdims=True)
        out_ref[0, :, cols] = (weigh(expo, v_all) / denom).astype(jnp.bfloat16)
        q = q_ref[1, :, cols]
        s = scores(q, k_all, noisy_bias)
        t = scores(q, k_own, own_bias)
        best = jnp.maximum(jnp.max(s, axis=1, keepdims=True), jnp.max(t, axis=1, keepdims=True))
        expo_s, expo_t = jnp.exp(s - best), jnp.exp(t - best)
        denom = jnp.sum(expo_s, axis=1, keepdims=True) + jnp.sum(expo_t, axis=1, keepdims=True)
        total = weigh(expo_s, v_all) + weigh(expo_t, v_own)
        out_ref[1, :, cols] = (total / denom).astype(jnp.bfloat16)


def attend(my_seq, queries, kv_clean, kv_noisy, tokens):
    seq = kv_clean.shape[0]
    _, rows, q_cols = queries.shape
    return pl.pallas_call(
        attend_kernel,
        out_shape=jax.ShapeDtypeStruct((2, rows, q_cols), jnp.bfloat16),
        grid_spec=pltpu.PrefetchScalarGridSpec(
            num_scalar_prefetch=1,
            grid=(rows // tokens,),
            in_specs=[
                pl.BlockSpec((2, tokens, q_cols), lambda i, s: (0, i, 0)),
                pl.BlockSpec((seq, 2, tokens, HD), lambda i, s: (0, 0, i, 0)),
                pl.BlockSpec((2, tokens, HD), lambda i, s: (0, i, 0)),
            ],
            out_specs=pl.BlockSpec((2, tokens, q_cols), lambda i, s: (0, i, 0)),
        ),
        compiler_params=pltpu.CompilerParams(vmem_limit_bytes=VMEM_BYTES),
    )(my_seq, queries, kv_clean, kv_noisy)


def combine_kernel(a_ref, w_ref, x_ref, mask_ref, embed_ref, clean_ref, noisy_ref):
    tp = a_ref.shape[0]
    clean = x_ref[0].astype(jnp.float32)
    noisy = jnp.where(mask_ref[...] == 1, embed_ref[...].astype(jnp.float32), clean)
    for stream, base, out in ((0, clean, clean_ref), (1, noisy, noisy_ref)):
        total = jnp.zeros(base.shape, jnp.float32)
        for t in range(tp):
            total = total + jnp.dot(a_ref[t, stream], w_ref[t], preferred_element_type=jnp.float32)
        out[0] = (base + total).astype(jnp.bfloat16)


def combine(attended, weight, clean_in, mask_col, mask_embed):
    tp, _, rows, q_cols = attended.shape
    docs, tokens, width = clean_in.shape
    block = pl.BlockSpec((1, tokens, width), lambda i: (i, 0, 0))
    out = jax.ShapeDtypeStruct(clean_in.shape, jnp.bfloat16)
    return pl.pallas_call(
        combine_kernel,
        out_shape=(out, out),
        grid=(docs,),
        in_specs=[
            pl.BlockSpec((tp, 2, tokens, q_cols), lambda i: (0, 0, i, 0)),
            pl.BlockSpec((tp, q_cols, width), lambda i: (0, 0, 0)),
            block,
            pl.BlockSpec((tokens, 1), lambda i: (i, 0)),
            pl.BlockSpec((1, width), lambda i: (0, 0)),
        ],
        out_specs=(block, block),
        compiler_params=pltpu.CompilerParams(vmem_limit_bytes=VMEM_BYTES),
    )(attended, weight, clean_in, mask_col, mask_embed.reshape(1, width))


def per_device(
    tp,
    seq,
    clean_in,
    noise_mask,
    mask_embed,
    norm_gain,
    q_weight,
    q_bias,
    k_weight,
    v_weight,
    v_bias,
    o_weight,
):
    docs, tokens, width = clean_in.shape
    q_cols = q_weight.shape[1]
    rows = docs * tokens
    lines = 4 if tp % 4 == 0 else 1
    cross = tp // lines
    seq_cross = 2 if seq % 2 == 0 else 1
    my_seq = lax.axis_index("seq")
    head = lax.axis_index("tp") * KVH // tp
    mask_col = noise_mask.reshape(rows, 1)
    own = jnp.concatenate(
        [clean_in.reshape(rows, width), jnp.broadcast_to(mask_embed[None, :], (PAD, width))], 0
    )
    dealt = jnp.transpose(o_weight.reshape(q_cols, tp, width), (1, 0, 2))
    whole, out_weight = first_gather(own, dealt, tp, seq, lines, cross)
    positions = (my_seq * tokens + jnp.arange(tokens)).astype(jnp.float32)
    cosine, sine = tables(positions)
    queries, kv_clean, kv_noisy = project(
        head.reshape(1), whole, mask_col, norm_gain, q_weight, q_bias, k_weight, v_weight, v_bias,
        cosine, sine,
    )
    kv_all = gather(kv_clean, "seq", seq // seq_cross, seq_cross, 1)
    attended = attend(my_seq.reshape(1), queries, kv_all, kv_noisy, tokens)
    spread = gather(attended, "tp", lines, cross, 2)
    return combine(spread, out_weight, clean_in, mask_col, mask_embed)


def solution(mesh):
    return jax.shard_map(
        functools.partial(per_device, mesh.shape["tp"], mesh.shape["seq"]),
        mesh=mesh,
        in_specs=(
            P(None, "seq", "tp"),
            P(None, "seq"),
            P("tp"),
            P(),
            P(None, "tp"),
            P("tp"),
            P(),
            P(),
            P(),
            P("tp", None),
        ),
        out_specs=(P(None, "seq", "tp"), P(None, "seq", "tp")),
        check_vma=False,
    )
```

```python
import functools
import math

import jax
import jax.numpy as jnp
from jax import lax
from jax.experimental import pallas as pl
from jax.experimental.pallas import tpu as pltpu
from jax.sharding import PartitionSpec as P

HD = 128
KVH = 8
BLOCK = 32
PAD = 16

eps = 1e-06
theta = 1000000.0
MESH = pl.DeviceIdType.MESH
VMEM_BYTES = 60 * 2**20


def tables(positions):
    half = HD // 2
    freqs = theta ** (-(jnp.arange(half).astype(jnp.float32) * 2.0) / HD)
    angles = positions[:, None] * freqs[None, :]
    cosine = jnp.cos(angles)
    sine = jnp.sin(angles)
    return jnp.concatenate([cosine, cosine], 1), jnp.concatenate([-sine, sine], 1)


def greet(groups):
    barrier = pltpu.get_barrier_semaphore()
    count = 0
    for axis, size in groups:
        me = lax.axis_index(axis)
        for step in range(1, size):
            pl.semaphore_signal(
                barrier, inc=1, device_id={axis: lax.rem(me + step, size)}, device_id_type=MESH
            )
        count += size - 1
    pl.semaphore_wait(barrier, count)


class Gather:
    def __init__(self, axis, lines, cross, own, out, send, recv, keep):
        self.axis, self.lines, self.cross = axis, lines, cross
        self.own, self.out, self.send, self.recv = own, out, send, recv
        me = lax.axis_index(axis)
        self.me, self.a, self.b = me, me // cross, lax.rem(me, cross)
        self.local = pltpu.make_async_copy(own, out.at[me], keep)
        self.started = []

    def copy(self, slot, way, device, src):
        return pltpu.make_async_remote_copy(
            src_ref=src,
            dst_ref=self.out.at[slot],
            send_sem=self.send.at[slot, way],
            recv_sem=self.recv.at[slot],
            device_id={self.axis: device},
            device_id_type=MESH,
        )

    def pass_on(self, slot, way, here, src=None):
        step = (self.cross, -self.cross, 1, -1)[way]
        inside = (
            self.a + 1 < self.lines, self.a > 0, self.b + 1 < self.cross, self.b > 0
        )[way]
        cond = inside if here is None else jnp.logical_and(here, inside)
        source = self.out.at[slot] if src is None else src

        @pl.when(cond)
        def _():
            self.copy(slot, way, self.me + step, source).start()

        self.started.append((slot, way, step, source, cond))

    def arrived(self, slot):
        self.copy(slot, 0, lax.rem(self.me + 1, self.lines * self.cross), self.out.at[slot]).wait_recv()

    def begin(self):
        for way in range(4):
            self.pass_on(self.me, way, None, self.own)
        self.local.start()

    def along(self, r):
        for sign in (-1, 1):
            src_a = self.a + sign * r
            here = src_a >= 0 if sign < 0 else src_a < self.lines
            slot = src_a * self.cross + self.b

            @pl.when(here)
            def _():
                self.arrived(slot)

            self.pass_on(slot, 0 if sign < 0 else 1, here)
            for way in (2, 3):
                self.pass_on(slot, way, here)

    def across(self):
        for r in range(1, self.cross):
            for sign in (-1, 1):
                src_b = self.b + sign * r
                here = src_b >= 0 if sign < 0 else src_b < self.cross
                for line in range(self.lines):
                    slot = line * self.cross + src_b

                    @pl.when(here)
                    def _():
                        self.arrived(slot)

                    if self.cross > 2:
                        self.pass_on(slot, 2 if sign < 0 else 3, here)

    def finish(self):
        for slot, way, step, source, cond in self.started:

            @pl.when(cond)
            def _():
                self.copy(slot, way, self.me + step, source).wait_send()

        self.local.wait()


def gather_kernel(axis, lines, cross, own, out, send, recv, keep):
    greet([(axis, lines * cross)])
    g = Gather(axis, lines, cross, own, out, send, recv, keep)
    g.begin()
    for r in range(1, lines):
        g.along(r)
    g.across()
    g.finish()


def gather(own, axis, lines, cross, collective_id):
    n = lines * cross
    return pl.pallas_call(
        functools.partial(gather_kernel, axis, lines, cross),
        out_shape=jax.ShapeDtypeStruct((n,) + own.shape, own.dtype),
        in_specs=[pl.BlockSpec(memory_space=pl.ANY)],
        out_specs=pl.BlockSpec(memory_space=pl.ANY),
        scratch_shapes=[
            pltpu.SemaphoreType.DMA((n, 4)),
            pltpu.SemaphoreType.DMA((n,)),
            pltpu.SemaphoreType.DMA,
        ],
        compiler_params=pltpu.CompilerParams(collective_id=collective_id, has_side_effects=True),
    )(own)


def first_kernel(
    tp, seq, lines, cross, own, weight, out, wout, send, recv, keep, wsend, wrecv, wkeep, xsend, xrecv
):
    greet([("tp", tp), ("seq", seq)])
    g = Gather("tp", lines, cross, own, out, send, recv, keep)
    g.begin()
    s = lax.axis_index("seq")
    rows = weight.shape[0] // seq
    cols = weight.shape[1] // lines
    piece = pl.ds(pl.multiple_of(s * rows, rows), rows)

    def deal(d):
        to = lax.rem(g.a + d, lines)
        return pltpu.make_async_remote_copy(
            src_ref=weight.at[piece, pl.ds(pl.multiple_of(to * cols, 128), cols)],
            dst_ref=wout.at[g.a, piece],
            send_sem=wsend.at[d],
            recv_sem=wrecv.at[d],
            device_id={"tp": to * cross + g.b},
            device_id_type=MESH,
        )

    def share(d, e):
        source = lax.rem(g.a + lines - d, lines)
        return pltpu.make_async_remote_copy(
            src_ref=wout.at[source, piece],
            dst_ref=wout.at[source, piece],
            send_sem=xsend.at[d, e],
            recv_sem=xrecv.at[d, e],
            device_id={"seq": lax.rem(s + e, seq)},
            device_id_type=MESH,
        )

    own_weight = pltpu.make_async_copy(
        weight.at[:, pl.ds(pl.multiple_of(g.a * cols, 128), cols)], wout.at[g.a], wkeep
    )
    own_weight.start()
    for d in range(1, lines):
        deal(d).start()
    g.along(1)
    for d in range(1, lines):
        deal(d).wait_recv()
        for e in range(1, seq):
            share(d, e).start()
    for r in range(2, lines):
        g.along(r)
    g.across()
    for d in range(1, lines):
        deal(d).wait_send()
        for e in range(1, seq):
            share(d, e).wait()
    own_weight.wait()
    g.finish()


def first_gather(own, weight, tp, seq, lines, cross):
    q_cols, d_model = weight.shape
    return pl.pallas_call(
        functools.partial(first_kernel, tp, seq, lines, cross),
        out_shape=(
            jax.ShapeDtypeStruct((tp,) + own.shape, own.dtype),
            jax.ShapeDtypeStruct((lines, q_cols, d_model // lines), weight.dtype),
        ),
        in_specs=[pl.BlockSpec(memory_space=pl.ANY)] * 2,
        out_specs=(pl.BlockSpec(memory_space=pl.ANY),) * 2,
        scratch_shapes=[
            pltpu.SemaphoreType.DMA((tp, 4)),
            pltpu.SemaphoreType.DMA((tp,)),
            pltpu.SemaphoreType.DMA,
            pltpu.SemaphoreType.DMA((lines,)),
            pltpu.SemaphoreType.DMA((lines,)),
            pltpu.SemaphoreType.DMA,
            pltpu.SemaphoreType.DMA((lines, seq)),
            pltpu.SemaphoreType.DMA((lines, seq)),
        ],
        compiler_params=pltpu.CompilerParams(collective_id=0, has_side_effects=True),
    )(own, weight)


def spin(values, cosine, sine):
    parts = []
    for start in range(0, values.shape[1], HD):
        head = values[:, start : start + HD]
        parts.append(head * cosine + pltpu.roll(head, HD // 2, 1) * sine)
    return jnp.concatenate(parts, 1) if len(parts) > 1 else parts[0]


def project_kernel(
    tp, head_ref, x_ref, m_ref, mask_ref, gain_ref, qw, qb, kw, vw, vb, cos_ref, sin_ref,
    q_out, kvc_out, kvn_out, qm, km, vm,
):
    del head_ref
    width = x_ref.shape[2]
    q_cols = qw.shape[1]

    def project(ref):
        rows = ref.shape[1]
        total = jnp.zeros((rows, 1), jnp.float32)
        for t in range(tp):
            part = ref[t].astype(jnp.float32)
            total = total + jnp.sum(part * part, axis=1, keepdims=True)
        scale = lax.rsqrt(total / (tp * width) + eps)
        q = jnp.zeros((rows, q_cols), jnp.float32)
        k = jnp.zeros((rows, HD), jnp.float32)
        v = jnp.zeros((rows, HD), jnp.float32)
        for t in range(tp):
            here = pl.ds(t * width, width)
            normed = (ref[t].astype(jnp.float32) * scale * gain_ref[t]).astype(jnp.bfloat16)
            q = q + jnp.dot(normed, qw[here, :], preferred_element_type=jnp.float32)
            k = k + jnp.dot(normed, kw[here, :], preferred_element_type=jnp.float32)
            v = v + jnp.dot(normed, vw[here, :], preferred_element_type=jnp.float32)
        return q + qb[...], k, v + vb[0]

    @pl.when(pl.program_id(0) == 0)
    def _():
        qm[...], km[...], vm[...] = project(m_ref)

    cosine, sine = cos_ref[...], sin_ref[...]
    rows = x_ref.shape[1]
    q, k, v = project(x_ref)
    q = spin(q, cosine, sine)
    k = spin(k, cosine, sine)
    masked = mask_ref[...] == 1
    q_mask = spin(jnp.broadcast_to(qm[0:1, :], (rows, q_cols)), cosine, sine)
    k_mask = spin(jnp.broadcast_to(km[0:1, :], (rows, HD)), cosine, sine)
    v_mask = jnp.broadcast_to(vm[0:1, :], (rows, HD))
    q_out[0] = q.astype(jnp.bfloat16)
    q_out[1] = jnp.where(masked, q_mask, q).astype(jnp.bfloat16)
    kvc_out[0] = k.astype(jnp.bfloat16)
    kvc_out[1] = v.astype(jnp.bfloat16)
    kvn_out[0] = jnp.where(masked, k_mask, k).astype(jnp.bfloat16)
    kvn_out[1] = jnp.where(masked, v_mask, v).astype(jnp.bfloat16)


def project(head, whole, mask_col, gain, q_weight, q_bias, k_weight, v_weight, v_bias, cosine, sine):
    tp, padded, width = whole.shape
    tokens = cosine.shape[0]
    rows = padded - PAD
    d_model, q_cols = q_weight.shape
    fixed = lambda *shape: pl.BlockSpec(shape, lambda i, h: (0,) * len(shape))
    return pl.pallas_call(
        functools.partial(project_kernel, tp),
        out_shape=(
            jax.ShapeDtypeStruct((2, rows, q_cols), jnp.bfloat16),
            jax.ShapeDtypeStruct((2, rows, HD), jnp.bfloat16),
            jax.ShapeDtypeStruct((2, rows, HD), jnp.bfloat16),
        ),
        grid_spec=pltpu.PrefetchScalarGridSpec(
            num_scalar_prefetch=1,
            grid=(rows // tokens,),
            in_specs=[
                pl.BlockSpec((tp, tokens, width), lambda i, h: (0, i, 0)),
                pl.BlockSpec((tp, PAD, width), lambda i, h: (0, rows // PAD, 0)),
                pl.BlockSpec((tokens, 1), lambda i, h: (i, 0)),
                fixed(tp, 1, width),
                fixed(d_model, q_cols),
                fixed(1, q_cols),
                pl.BlockSpec((d_model, HD), lambda i, h: (0, h[0])),
                pl.BlockSpec((d_model, HD), lambda i, h: (0, h[0])),
                pl.BlockSpec((1, 1, HD), lambda i, h: (h[0], 0, 0)),
                fixed(tokens, HD),
                fixed(tokens, HD),
            ],
            out_specs=(
                pl.BlockSpec((2, tokens, q_cols), lambda i, h: (0, i, 0)),
                pl.BlockSpec((2, tokens, HD), lambda i, h: (0, i, 0)),
                pl.BlockSpec((2, tokens, HD), lambda i, h: (0, i, 0)),
            ),
            scratch_shapes=[
                pltpu.VMEM((PAD, q_cols), jnp.float32),
                pltpu.VMEM((PAD, HD), jnp.float32),
                pltpu.VMEM((PAD, HD), jnp.float32),
            ],
        ),
        compiler_params=pltpu.CompilerParams(vmem_limit_bytes=VMEM_BYTES),
    )(
        head, whole, whole, mask_col, gain.reshape(tp, 1, width), q_weight, q_bias.reshape(1, -1),
        k_weight, v_weight, v_bias.reshape(-1, 1, HD), cosine, sine,
    )


def finish_kernel(
    tp, lines, cross, q_ref, kv_ref, kvn_ref, w_ref, x_ref, mask_ref, embed_ref, clean_ref, noisy_ref,
    heads_ref, total_ref, leave_ref, come_ref, send, recv, psend, precv,
):
    greet([("tp", tp)])
    me = lax.axis_index("tp")
    a, b = me // cross, lax.rem(me, cross)
    seq, _, docs, tokens, _ = kv_ref.shape
    q_cols = q_ref.shape[3]
    width = x_ref.shape[2]
    keys = seq * tokens
    scale = 1.0 / math.sqrt(HD)

    def blocks(count, axis, start):
        return (start + lax.broadcasted_iota(jnp.int32, (tokens, count), axis)) // BLOCK

    q_block = blocks(keys, 0, lax.axis_index("seq") * tokens)
    k_block = blocks(keys, 1, 0)
    clean_bias = jnp.where(k_block <= q_block, 0.0, -1e30)
    noisy_bias = jnp.where(k_block < q_block, 0.0, -1e30)
    own_bias = jnp.where(blocks(tokens, 1, 0) == blocks(tokens, 0, 0), 0.0, -1e30)

    def scores(q, k, bias):
        dims = (((1,), (1,)), ((), ()))
        return lax.dot_general(q, k, dims, preferred_element_type=jnp.float32) * scale + bias

    def weigh(expo, v):
        return jnp.dot(expo.astype(jnp.bfloat16), v, preferred_element_type=jnp.float32)

    def pass_on(d, slot, way):
        return pltpu.make_async_remote_copy(
            src_ref=heads_ref.at[d, slot],
            dst_ref=heads_ref.at[d, slot],
            send_sem=send.at[d, slot, way],
            recv_sem=recv.at[d, slot],
            device_id={"tp": lax.rem(me + (cross, tp - cross)[way], tp)},
            device_id_type=MESH,
        )

    more = (a + 1 < lines, a > 0)

    def attend(d, carry):
        k_all = kv_ref[:, 0, d].reshape(keys, HD)
        v_all = kv_ref[:, 1, d].reshape(keys, HD)
        k_own, v_own = kvn_ref[0, d], kvn_ref[1, d]
        for h in range(q_cols // HD):
            cols = pl.ds(h * HD, HD)
            s = scores(q_ref[0, d, :, cols], k_all, clean_bias)
            expo = jnp.exp(s - jnp.max(s, axis=1, keepdims=True))
            denom = jnp.sum(expo, axis=1, keepdims=True)
            heads_ref[d, a, 0, :, cols] = (weigh(expo, v_all) / denom).astype(jnp.bfloat16)
            q = q_ref[1, d, :, cols]
            s = scores(q, k_all, noisy_bias)
            t = scores(q, k_own, own_bias)
            best = jnp.maximum(jnp.max(s, axis=1, keepdims=True), jnp.max(t, axis=1, keepdims=True))
            expo_s, expo_t = jnp.exp(s - best), jnp.exp(t - best)
            denom = jnp.sum(expo_s, axis=1, keepdims=True) + jnp.sum(expo_t, axis=1, keepdims=True)
            total = weigh(expo_s, v_all) + weigh(expo_t, v_own)
            heads_ref[d, a, 1, :, cols] = (total / denom).astype(jnp.bfloat16)
        for way in range(2):

            @pl.when(more[way])
            def _():
                pass_on(d, a, way).start()

        return carry

    lax.fori_loop(0, docs, attend, 0)

    def along(r, d):
        for way, here, slot in ((0, a - r >= 0, a - r), (1, a + r < lines, a + r)):

            @pl.when(here)
            def _():
                pass_on(d, slot, way).wait_recv()

            @pl.when(jnp.logical_and(here, more[way]))
            def _():
                pass_on(d, slot, way).start()

    for r in range(1, lines - 1):
        lax.fori_loop(0, docs, lambda d, carry: (along(r, d), carry)[1], 0)

    def partial(d, e):
        return pltpu.make_async_remote_copy(
            src_ref=leave_ref.at[d, e],
            dst_ref=come_ref.at[d, e],
            send_sem=psend.at[d, e],
            recv_sem=precv.at[d, e],
            device_id={"tp": a * cross + lax.rem(b + e, cross)},
            device_id_type=MESH,
        )

    def multiply(d, carry):
        along(lines - 1, d)
        for stream in range(2):
            total = jnp.zeros((tokens, cross * width), jnp.float32)
            for line in range(lines):
                total = total + jnp.dot(
                    heads_ref[d, line, stream], w_ref[line], preferred_element_type=jnp.float32
                )
            for target in range(cross):
                part = total[:, target * width : (target + 1) * width]

                @pl.when(b == target)
                def _():
                    total_ref[d, stream] = part

                @pl.when(b != target)
                def _():
                    leave_ref[d, lax.rem(target - b + cross, cross), stream] = part.astype(
                        jnp.bfloat16
                    )

        for e in range(1, cross):
            partial(d, e).start()
        return carry

    lax.fori_loop(0, docs, multiply, 0)

    def close(d, carry):
        clean = x_ref[d].astype(jnp.float32)
        noisy = jnp.where(mask_ref[d] == 1, embed_ref[...].astype(jnp.float32), clean)
        for e in range(1, cross):
            partial(d, e).wait_recv()
        for stream, base, out in ((0, clean, clean_ref), (1, noisy, noisy_ref)):
            total = total_ref[d, stream]
            for e in range(1, cross):
                total = total + come_ref[d, e, stream].astype(jnp.float32)
            out[d] = (base + total).astype(jnp.bfloat16)
        for e in range(1, cross):
            partial(d, e).wait_send()
        for r in range(lines):
            for way, here, slot in ((0, a - r >= 0, a - r), (1, a + r < lines, a + r)):

                @pl.when(jnp.logical_and(here, more[way]))
                def _():
                    pass_on(d, slot, way).wait_send()

        return carry

    lax.fori_loop(0, docs, close, 0)


def finish(queries, kv_all, kv_noisy, weight, clean_in, mask_col, mask_embed, tp, lines, cross):
    docs, tokens, width = clean_in.shape
    q_cols = queries.shape[2]
    seq = kv_all.shape[0]
    out = jax.ShapeDtypeStruct(clean_in.shape, jnp.bfloat16)
    vmem = pl.BlockSpec(memory_space=pltpu.VMEM)
    dma = pltpu.SemaphoreType.DMA
    return pl.pallas_call(
        functools.partial(finish_kernel, tp, lines, cross),
        out_shape=(out, out),
        in_specs=[vmem] * 7,
        out_specs=(vmem, vmem),
        scratch_shapes=[
            pltpu.VMEM((docs, lines, 2, tokens, q_cols), jnp.bfloat16),
            pltpu.VMEM((docs, 2, tokens, width), jnp.float32),
            pltpu.VMEM((docs, cross, 2, tokens, width), jnp.bfloat16),
            pltpu.VMEM((docs, cross, 2, tokens, width), jnp.bfloat16),
            dma((docs, lines, 2)),
            dma((docs, lines)),
            dma((docs, cross)),
            dma((docs, cross)),
        ],
        compiler_params=pltpu.CompilerParams(
            collective_id=2, has_side_effects=True, vmem_limit_bytes=VMEM_BYTES
        ),
    )(
        queries.reshape(2, docs, tokens, q_cols),
        kv_all.reshape(seq, 2, docs, tokens, HD),
        kv_noisy.reshape(2, docs, tokens, HD),
        weight,
        clean_in,
        mask_col.reshape(docs, tokens, 1),
        mask_embed.reshape(1, width),
    )


def per_device(
    tp,
    seq,
    clean_in,
    noise_mask,
    mask_embed,
    norm_gain,
    q_weight,
    q_bias,
    k_weight,
    v_weight,
    v_bias,
    o_weight,
):
    docs, tokens, width = clean_in.shape
    rows = docs * tokens
    lines = 4 if tp % 4 == 0 else 1
    cross = tp // lines
    seq_cross = 2 if seq % 2 == 0 else 1
    my_seq = lax.axis_index("seq")
    head = lax.axis_index("tp") * KVH // tp
    mask_col = noise_mask.reshape(rows, 1)
    own = jnp.concatenate(
        [clean_in.reshape(rows, width), jnp.broadcast_to(mask_embed[None, :], (PAD, width))], 0
    )
    whole, out_weight = first_gather(own, o_weight, tp, seq, lines, cross)
    positions = (my_seq * tokens + jnp.arange(tokens)).astype(jnp.float32)
    cosine, sine = tables(positions)
    queries, kv_clean, kv_noisy = project(
        head.reshape(1), whole, mask_col, norm_gain, q_weight, q_bias, k_weight, v_weight, v_bias,
        cosine, sine,
    )
    kv_all = gather(kv_clean, "seq", seq // seq_cross, seq_cross, 1)
    return finish(
        queries, kv_all, kv_noisy, out_weight, clean_in, mask_col, mask_embed, tp, lines, cross
    )


def solution(mesh):
    return jax.shard_map(
        functools.partial(per_device, mesh.shape["tp"], mesh.shape["seq"]),
        mesh=mesh,
        in_specs=(
            P(None, "seq", "tp"),
            P(None, "seq"),
            P("tp"),
            P(),
            P(None, "tp"),
            P("tp"),
            P(),
            P(),
            P(),
            P("tp", None),
        ),
        out_specs=(P(None, "seq", "tp"), P(None, "seq", "tp")),
        check_vma=False,
    )
```

```python
import functools
import math

import jax
import jax.numpy as jnp
from jax import lax
from jax.experimental import pallas as pl
from jax.experimental.pallas import tpu as pltpu
from jax.sharding import PartitionSpec as P

HD = 128
KVH = 8
BLOCK = 32
PAD = 16

eps = 1e-06
theta = 1000000.0
MESH = pl.DeviceIdType.MESH
VMEM_BYTES = 60 * 2**20


def tables(positions):
    half = HD // 2
    freqs = theta ** (-(jnp.arange(half).astype(jnp.float32) * 2.0) / HD)
    angles = positions[:, None] * freqs[None, :]
    cosine = jnp.cos(angles)
    sine = jnp.sin(angles)
    return jnp.concatenate([cosine, cosine], 1), jnp.concatenate([-sine, sine], 1)


def greet(groups):
    barrier = pltpu.get_barrier_semaphore()
    count = 0
    for axis, size in groups:
        me = lax.axis_index(axis)
        for step in range(1, size):
            pl.semaphore_signal(
                barrier, inc=1, device_id={axis: lax.rem(me + step, size)}, device_id_type=MESH
            )
        count += size - 1
    pl.semaphore_wait(barrier, count)


def spin(values, cosine, sine):
    parts = []
    for start in range(0, values.shape[1], HD):
        head = values[:, start : start + HD]
        parts.append(head * cosine + pltpu.roll(head, HD // 2, 1) * sine)
    return jnp.concatenate(parts, 1) if len(parts) > 1 else parts[0]


def first_kernel(
    tp, seq, lines, cross,
    x_ref, embed_ref, mask_ref, gain_ref, qw, qb, kw_any, vw_any, vb, cos_ref, sin_ref, weight,
    q_out, kv_out, kvn_out, wout,
    held, marks, kw, vw, qm, km, vm,
    send, recv, msend, mrecv, kvsend, kvrecv, wsend, wrecv, xsend, xrecv, keep,
):
    greet([("tp", tp), ("seq", seq)])
    me = lax.axis_index("tp")
    s = lax.axis_index("seq")
    a, b = me // cross, lax.rem(me, cross)
    docs, tokens, width = x_ref.shape
    q_cols = qw.shape[1]
    head = pl.ds(pl.multiple_of(me * KVH // tp * HD, HD), HD)
    steps = (cross, tp - cross, 1, tp - 1)
    more = (a + 1 < lines, a > 0, b + 1 < cross, b > 0)

    def pass_on(d, slot, way):
        return pltpu.make_async_remote_copy(
            src_ref=held.at[d, slot],
            dst_ref=held.at[d, slot],
            send_sem=send.at[d, slot, way],
            recv_sem=recv.at[d, slot],
            device_id={"tp": lax.rem(me + steps[way], tp)},
            device_id_type=MESH,
        )

    def mark(e):
        return pltpu.make_async_remote_copy(
            src_ref=marks.at[me],
            dst_ref=marks.at[me],
            send_sem=msend.at[e],
            recv_sem=mrecv.at[e],
            device_id={"tp": lax.rem(me + e, tp)},
            device_id_type=MESH,
        )

    def tell(d, e):
        return pltpu.make_async_remote_copy(
            src_ref=kv_out.at[d, s],
            dst_ref=kv_out.at[d, s],
            send_sem=kvsend.at[d, e],
            recv_sem=kvrecv.at[d, e],
            device_id={"seq": lax.rem(s + e, seq)},
            device_id_type=MESH,
        )

    rows = weight.shape[0] // seq
    cols = weight.shape[1] // lines
    piece = pl.ds(pl.multiple_of(s * rows, rows), rows)

    def deal(e):
        to = lax.rem(a + e, lines)
        return pltpu.make_async_remote_copy(
            src_ref=weight.at[piece, pl.ds(pl.multiple_of(to * cols, 128), cols)],
            dst_ref=wout.at[a, piece],
            send_sem=wsend.at[e],
            recv_sem=wrecv.at[e],
            device_id={"tp": to * cross + b},
            device_id_type=MESH,
        )

    def share(e, f):
        source = lax.rem(a + lines - e, lines)
        return pltpu.make_async_remote_copy(
            src_ref=wout.at[source, piece],
            dst_ref=wout.at[source, piece],
            send_sem=xsend.at[e, f],
            recv_sem=xrecv.at[e, f],
            device_id={"seq": lax.rem(s + f, seq)},
            device_id_type=MESH,
        )

    stays = (
        pltpu.make_async_copy(
            weight.at[:, pl.ds(pl.multiple_of(a * cols, 128), cols)], wout.at[a], keep.at[0]
        ),
        pltpu.make_async_copy(kw_any.at[:, head], kw, keep.at[1]),
        pltpu.make_async_copy(vw_any.at[:, head], vw, keep.at[2]),
    )
    marks[me] = jnp.broadcast_to(embed_ref[...], (PAD, width))
    for e in range(1, tp):
        mark(e).start()
    for copy in stays:
        copy.start()

    def places(r):
        return ((0, a - r >= 0, a - r), (1, a + r < lines, a + r))

    def along(r, d):
        for way, here, line in places(r):
            slot = line * cross + b

            @pl.when(here)
            def _():
                pass_on(d, slot, way).wait_recv()

            for out in (way, 2, 3):

                @pl.when(jnp.logical_and(here, more[out]))
                def _():
                    pass_on(d, slot, out).start()

    def columns(r):
        return ((2, b - r >= 0, b - r), (3, b + r < cross, b + r))

    def across(d):
        for r in range(1, cross):
            for way, here, col in columns(r):
                for line in range(lines):

                    @pl.when(here)
                    def _():
                        pass_on(d, line * cross + col, way).wait_recv()

                    if cross > 2:

                        @pl.when(jnp.logical_and(here, more[way]))
                        def _():
                            pass_on(d, line * cross + col, way).start()

    def project(part_of):
        rows = part_of(0).shape[0]
        total = jnp.zeros((rows, 1), jnp.float32)
        for t in range(tp):
            part = part_of(t).astype(jnp.float32)
            total = total + jnp.sum(part * part, axis=1, keepdims=True)
        scale = lax.rsqrt(total / (tp * width) + eps)
        q = jnp.zeros((rows, q_cols), jnp.float32)
        k = jnp.zeros((rows, HD), jnp.float32)
        v = jnp.zeros((rows, HD), jnp.float32)
        for t in range(tp):
            here = pl.ds(t * width, width)
            normed = (part_of(t).astype(jnp.float32) * scale * gain_ref[t]).astype(jnp.bfloat16)
            q = q + jnp.dot(normed, qw[here, :], preferred_element_type=jnp.float32)
            k = k + jnp.dot(normed, kw[here, :], preferred_element_type=jnp.float32)
            v = v + jnp.dot(normed, vw[here, :], preferred_element_type=jnp.float32)
        return q + qb[...], k, v + vb[me * KVH // tp]

    def wave(step, carry):
        @pl.when(step < docs)
        def _():
            held[step, me] = x_ref[step]
            for way in range(4):

                @pl.when(more[way])
                def _():
                    pass_on(step, me, way).start()

        @pl.when(step == 1)
        def _():
            for e in range(1, lines):
                deal(e).start()

        for r in range(1, lines):

            @pl.when(jnp.logical_and(step >= r, step < docs + r))
            def _():
                along(r, step - r)

        @pl.when(step == lines)
        def _():
            for e in range(1, tp):
                mark(e).wait_recv()
            stays[1].wait()
            stays[2].wait()
            qm[...], km[...], vm[...] = project(lambda t: marks[t])

        @pl.when(step >= lines)
        def _():
            d = step - lines
            across(d)
            cosine, sine = cos_ref[...], sin_ref[...]
            q, k, v = project(lambda t: held[d, t])
            q = spin(q, cosine, sine)
            k = spin(k, cosine, sine)
            kv_out[d, s, 0] = k.astype(jnp.bfloat16)
            kv_out[d, s, 1] = v.astype(jnp.bfloat16)
            for e in range(1, seq):
                tell(d, e).start()
            masked = mask_ref[d] == 1
            q_mask = spin(jnp.broadcast_to(qm[0:1, :], (tokens, q_cols)), cosine, sine)
            k_mask = spin(jnp.broadcast_to(km[0:1, :], (tokens, HD)), cosine, sine)
            v_mask = jnp.broadcast_to(vm[0:1, :], (tokens, HD))
            q_out[0, d] = q.astype(jnp.bfloat16)
            q_out[1, d] = jnp.where(masked, q_mask, q).astype(jnp.bfloat16)
            kvn_out[0, d] = jnp.where(masked, k_mask, k).astype(jnp.bfloat16)
            kvn_out[1, d] = jnp.where(masked, v_mask, v).astype(jnp.bfloat16)

        @pl.when(step == lines)
        def _():
            for e in range(1, lines):
                deal(e).wait_recv()
                for f in range(1, seq):
                    share(e, f).start()

        return carry

    lax.fori_loop(0, docs + lines, wave, 0)

    def close(d, carry):
        for e in range(1, seq):
            tell(d, e).wait()
        for r in range(lines):
            for way, here, line in places(r):
                slot = line * cross + b
                outs = (way, way + 2) if r == 0 else (way, 2, 3)
                for out in outs:

                    @pl.when(jnp.logical_and(here, more[out]))
                    def _():
                        pass_on(d, slot, out).wait_send()

        if cross > 2:
            for r in range(1, cross):
                for way, here, col in columns(r):
                    for line in range(lines):

                        @pl.when(jnp.logical_and(here, more[way]))
                        def _():
                            pass_on(d, line * cross + col, way).wait_send()

        return carry

    lax.fori_loop(0, docs, close, 0)
    for e in range(1, tp):
        mark(e).wait_send()
    for e in range(1, lines):
        deal(e).wait_send()
        for f in range(1, seq):
            share(e, f).wait()
    stays[0].wait()


def first(
    clean_in, mask_col, mask_embed, gain, q_weight, q_bias, k_weight, v_weight, v_bias,
    cosine, sine, weight, tp, seq, lines, cross,
):
    docs, tokens, width = clean_in.shape
    d_model, q_cols = q_weight.shape
    vmem = pl.BlockSpec(memory_space=pltpu.VMEM)
    anywhere = pl.BlockSpec(memory_space=pl.ANY)
    dma = pltpu.SemaphoreType.DMA
    bf16 = jnp.bfloat16
    return pl.pallas_call(
        functools.partial(first_kernel, tp, seq, lines, cross),
        out_shape=(
            jax.ShapeDtypeStruct((2, docs, tokens, q_cols), bf16),
            jax.ShapeDtypeStruct((docs, seq, 2, tokens, HD), bf16),
            jax.ShapeDtypeStruct((2, docs, tokens, HD), bf16),
            jax.ShapeDtypeStruct((lines, q_cols, d_model // lines), bf16),
        ),
        in_specs=[vmem] * 6 + [anywhere] * 2 + [vmem] * 3 + [anywhere],
        out_specs=(vmem, vmem, vmem, anywhere),
        scratch_shapes=[
            pltpu.VMEM((docs, tp, tokens, width), bf16),
            pltpu.VMEM((tp, PAD, width), bf16),
            pltpu.VMEM((d_model, HD), bf16),
            pltpu.VMEM((d_model, HD), bf16),
            pltpu.VMEM((PAD, q_cols), jnp.float32),
            pltpu.VMEM((PAD, HD), jnp.float32),
            pltpu.VMEM((PAD, HD), jnp.float32),
            dma((docs, tp, 4)),
            dma((docs, tp)),
            dma((tp,)),
            dma((tp,)),
            dma((docs, seq)),
            dma((docs, seq)),
            dma((lines,)),
            dma((lines,)),
            dma((lines, seq)),
            dma((lines, seq)),
            dma((3,)),
        ],
        compiler_params=pltpu.CompilerParams(
            collective_id=0, has_side_effects=True, vmem_limit_bytes=VMEM_BYTES
        ),
    )(
        clean_in, mask_embed.reshape(1, width), mask_col, gain.reshape(tp, 1, width), q_weight,
        q_bias.reshape(1, -1), k_weight, v_weight, v_bias.reshape(-1, 1, HD), cosine, sine, weight,
    )


def finish_kernel(
    tp, lines, cross, q_ref, kv_ref, kvn_ref, w_ref, x_ref, mask_ref, embed_ref, clean_ref, noisy_ref,
    heads_ref, total_ref, leave_ref, come_ref, send, recv, psend, precv,
):
    greet([("tp", tp)])
    me = lax.axis_index("tp")
    a, b = me // cross, lax.rem(me, cross)
    docs, seq, _, tokens, _ = kv_ref.shape
    q_cols = q_ref.shape[3]
    width = x_ref.shape[2]
    keys = seq * tokens
    scale = 1.0 / math.sqrt(HD)

    def blocks(count, axis, start):
        return (start + lax.broadcasted_iota(jnp.int32, (tokens, count), axis)) // BLOCK

    q_block = blocks(keys, 0, lax.axis_index("seq") * tokens)
    k_block = blocks(keys, 1, 0)
    clean_bias = jnp.where(k_block <= q_block, 0.0, -1e30)
    noisy_bias = jnp.where(k_block < q_block, 0.0, -1e30)
    own_bias = jnp.where(blocks(tokens, 1, 0) == blocks(tokens, 0, 0), 0.0, -1e30)

    def scores(q, k, bias):
        dims = (((1,), (1,)), ((), ()))
        return lax.dot_general(q, k, dims, preferred_element_type=jnp.float32) * scale + bias

    def weigh(expo, v):
        return jnp.dot(expo.astype(jnp.bfloat16), v, preferred_element_type=jnp.float32)

    def pass_on(d, slot, way):
        return pltpu.make_async_remote_copy(
            src_ref=heads_ref.at[d, slot],
            dst_ref=heads_ref.at[d, slot],
            send_sem=send.at[d, slot, way],
            recv_sem=recv.at[d, slot],
            device_id={"tp": lax.rem(me + (cross, tp - cross)[way], tp)},
            device_id_type=MESH,
        )

    more = (a + 1 < lines, a > 0)

    def attend(d):
        k_all = kv_ref[d, :, 0].reshape(keys, HD)
        v_all = kv_ref[d, :, 1].reshape(keys, HD)
        k_own, v_own = kvn_ref[0, d], kvn_ref[1, d]
        for h in range(q_cols // HD):
            cols = pl.ds(h * HD, HD)
            s = scores(q_ref[0, d, :, cols], k_all, clean_bias)
            expo = jnp.exp(s - jnp.max(s, axis=1, keepdims=True))
            denom = jnp.sum(expo, axis=1, keepdims=True)
            heads_ref[d, a, 0, :, cols] = (weigh(expo, v_all) / denom).astype(jnp.bfloat16)
            q = q_ref[1, d, :, cols]
            s = scores(q, k_all, noisy_bias)
            t = scores(q, k_own, own_bias)
            best = jnp.maximum(jnp.max(s, axis=1, keepdims=True), jnp.max(t, axis=1, keepdims=True))
            expo_s, expo_t = jnp.exp(s - best), jnp.exp(t - best)
            denom = jnp.sum(expo_s, axis=1, keepdims=True) + jnp.sum(expo_t, axis=1, keepdims=True)
            total = weigh(expo_s, v_all) + weigh(expo_t, v_own)
            heads_ref[d, a, 1, :, cols] = (total / denom).astype(jnp.bfloat16)
        for way in range(2):

            @pl.when(more[way])
            def _():
                pass_on(d, a, way).start()

    def along(r, d):
        for way, here, slot in ((0, a - r >= 0, a - r), (1, a + r < lines, a + r)):

            @pl.when(here)
            def _():
                pass_on(d, slot, way).wait_recv()

            @pl.when(jnp.logical_and(here, more[way]))
            def _():
                pass_on(d, slot, way).start()

    def partial(d, e):
        return pltpu.make_async_remote_copy(
            src_ref=leave_ref.at[d, e],
            dst_ref=come_ref.at[d, e],
            send_sem=psend.at[d, e],
            recv_sem=precv.at[d, e],
            device_id={"tp": a * cross + lax.rem(b + e, cross)},
            device_id_type=MESH,
        )

    def multiply(d):
        for stream in range(2):
            total = jnp.zeros((tokens, cross * width), jnp.float32)
            for line in range(lines):
                total = total + jnp.dot(
                    heads_ref[d, line, stream], w_ref[line], preferred_element_type=jnp.float32
                )
            for target in range(cross):
                part = total[:, target * width : (target + 1) * width]

                @pl.when(b == target)
                def _():
                    total_ref[d, stream] = part

                @pl.when(b != target)
                def _():
                    leave_ref[d, lax.rem(target - b + cross, cross), stream] = part.astype(
                        jnp.bfloat16
                    )

        for e in range(1, cross):
            partial(d, e).start()

    def wave(step, carry):
        @pl.when(step < docs)
        def _():
            attend(step)

        for r in range(1, lines):

            @pl.when(jnp.logical_and(step >= r, step < docs + r))
            def _():
                along(r, step - r)

        @pl.when(step >= lines - 1)
        def _():
            multiply(step - (lines - 1))

        return carry

    lax.fori_loop(0, docs + lines - 1, wave, 0)

    def close(d, carry):
        clean = x_ref[d].astype(jnp.float32)
        noisy = jnp.where(mask_ref[d] == 1, embed_ref[...].astype(jnp.float32), clean)
        for e in range(1, cross):
            partial(d, e).wait_recv()
        for stream, base, out in ((0, clean, clean_ref), (1, noisy, noisy_ref)):
            total = total_ref[d, stream]
            for e in range(1, cross):
                total = total + come_ref[d, e, stream].astype(jnp.float32)
            out[d] = (base + total).astype(jnp.bfloat16)
        for e in range(1, cross):
            partial(d, e).wait_send()
        for r in range(lines):
            for way, here, slot in ((0, a - r >= 0, a - r), (1, a + r < lines, a + r)):

                @pl.when(jnp.logical_and(here, more[way]))
                def _():
                    pass_on(d, slot, way).wait_send()

        return carry

    lax.fori_loop(0, docs, close, 0)


def finish(queries, kv_all, kv_noisy, weight, clean_in, mask_col, mask_embed, tp, lines, cross):
    docs, tokens, width = clean_in.shape
    q_cols = queries.shape[3]
    out = jax.ShapeDtypeStruct(clean_in.shape, jnp.bfloat16)
    vmem = pl.BlockSpec(memory_space=pltpu.VMEM)
    dma = pltpu.SemaphoreType.DMA
    return pl.pallas_call(
        functools.partial(finish_kernel, tp, lines, cross),
        out_shape=(out, out),
        in_specs=[vmem] * 7,
        out_specs=(vmem, vmem),
        scratch_shapes=[
            pltpu.VMEM((docs, lines, 2, tokens, q_cols), jnp.bfloat16),
            pltpu.VMEM((docs, 2, tokens, width), jnp.float32),
            pltpu.VMEM((docs, cross, 2, tokens, width), jnp.bfloat16),
            pltpu.VMEM((docs, cross, 2, tokens, width), jnp.bfloat16),
            dma((docs, lines, 2)),
            dma((docs, lines)),
            dma((docs, cross)),
            dma((docs, cross)),
        ],
        compiler_params=pltpu.CompilerParams(
            collective_id=2, has_side_effects=True, vmem_limit_bytes=VMEM_BYTES
        ),
    )(
        queries,
        kv_all,
        kv_noisy,
        weight,
        clean_in,
        mask_col,
        mask_embed.reshape(1, width),
    )


def per_device(
    tp,
    seq,
    clean_in,
    noise_mask,
    mask_embed,
    norm_gain,
    q_weight,
    q_bias,
    k_weight,
    v_weight,
    v_bias,
    o_weight,
):
    docs, tokens, _ = clean_in.shape
    lines = 4 if tp % 4 == 0 else 1
    cross = tp // lines
    my_seq = lax.axis_index("seq")
    mask_col = noise_mask.reshape(docs, tokens, 1)
    positions = (my_seq * tokens + jnp.arange(tokens)).astype(jnp.float32)
    cosine, sine = tables(positions)
    queries, kv_all, kv_noisy, out_weight = first(
        clean_in, mask_col, mask_embed, norm_gain, q_weight, q_bias, k_weight, v_weight, v_bias,
        cosine, sine, o_weight, tp, seq, lines, cross,
    )
    return finish(
        queries, kv_all, kv_noisy, out_weight, clean_in, mask_col, mask_embed, tp, lines, cross
    )


def solution(mesh):
    return jax.shard_map(
        functools.partial(per_device, mesh.shape["tp"], mesh.shape["seq"]),
        mesh=mesh,
        in_specs=(
            P(None, "seq", "tp"),
            P(None, "seq"),
            P("tp"),
            P(),
            P(None, "tp"),
            P("tp"),
            P(),
            P(),
            P(),
            P("tp", None),
        ),
        out_specs=(P(None, "seq", "tp"), P(None, "seq", "tp")),
        check_vma=False,
    )
```

```python
import functools
import math

import jax
import jax.numpy as jnp
from jax import lax
from jax.experimental import pallas as pl
from jax.experimental.pallas import tpu as pltpu
from jax.sharding import PartitionSpec as P

HD = 128
KVH = 8
BLOCK = 32
PAD = 16

eps = 1e-06
theta = 1000000.0
MESH = pl.DeviceIdType.MESH
VMEM_BYTES = 60 * 2**20


def tables(positions):
    half = HD // 2
    freqs = theta ** (-(jnp.arange(half).astype(jnp.float32) * 2.0) / HD)
    angles = positions[:, None] * freqs[None, :]
    cosine = jnp.cos(angles)
    sine = jnp.sin(angles)
    return jnp.concatenate([cosine, cosine], 1), jnp.concatenate([-sine, sine], 1)


def greet(groups):
    barrier = pltpu.get_barrier_semaphore()
    count = 0
    for axis, size in groups:
        me = lax.axis_index(axis)
        for step in range(1, size):
            pl.semaphore_signal(
                barrier, inc=1, device_id={axis: lax.rem(me + step, size)}, device_id_type=MESH
            )
        count += size - 1
    pl.semaphore_wait(barrier, count)


def spin(values, cosine, sine):
    parts = []
    for start in range(0, values.shape[1], HD):
        head = values[:, start : start + HD]
        parts.append(head * cosine + pltpu.roll(head, HD // 2, 1) * sine)
    return jnp.concatenate(parts, 1) if len(parts) > 1 else parts[0]


def first_kernel(
    tp, seq, lines, cross,
    x_ref, embed_ref, mask_ref, gain_ref, qw, qb, kw_any, vw_any, vb, cos_ref, sin_ref, weight,
    q_out, kv_out, kvn_out, wout,
    held, marks, kw, vw, qm, km, vm,
    send, recv, msend, mrecv, kvsend, kvrecv, wsend, wrecv, xsend, xrecv, keep,
):
    greet([("tp", tp), ("seq", seq)])
    me = lax.axis_index("tp")
    s = lax.axis_index("seq")
    a, b = me // cross, lax.rem(me, cross)
    docs, tokens, width = x_ref.shape
    q_cols = qw.shape[1]
    head = pl.ds(pl.multiple_of(me * KVH // tp * HD, HD), HD)
    steps = (cross, tp - cross, 1, tp - 1)
    more = (a + 1 < lines, a > 0, b + 1 < cross, b > 0)

    def pass_on(d, slot, way):
        return pltpu.make_async_remote_copy(
            src_ref=held.at[d, slot],
            dst_ref=held.at[d, slot],
            send_sem=send.at[d, slot, way],
            recv_sem=recv.at[d, slot],
            device_id={"tp": lax.rem(me + steps[way], tp)},
            device_id_type=MESH,
        )

    def mark(e):
        return pltpu.make_async_remote_copy(
            src_ref=marks.at[me],
            dst_ref=marks.at[me],
            send_sem=msend.at[e],
            recv_sem=mrecv.at[e],
            device_id={"tp": lax.rem(me + e, tp)},
            device_id_type=MESH,
        )

    def tell(d, e):
        return pltpu.make_async_remote_copy(
            src_ref=kv_out.at[d, s],
            dst_ref=kv_out.at[d, s],
            send_sem=kvsend.at[d, e],
            recv_sem=kvrecv.at[d, e],
            device_id={"seq": lax.rem(s + e, seq)},
            device_id_type=MESH,
        )

    rows = weight.shape[0] // seq
    cols = weight.shape[1] // lines
    piece = pl.ds(pl.multiple_of(s * rows, rows), rows)

    def deal(e):
        to = lax.rem(a + e, lines)
        return pltpu.make_async_remote_copy(
            src_ref=weight.at[piece, pl.ds(pl.multiple_of(to * cols, 128), cols)],
            dst_ref=wout.at[a, piece],
            send_sem=wsend.at[e],
            recv_sem=wrecv.at[e],
            device_id={"tp": to * cross + b},
            device_id_type=MESH,
        )

    def share(e, f):
        source = lax.rem(a + lines - e, lines)
        return pltpu.make_async_remote_copy(
            src_ref=wout.at[source, piece],
            dst_ref=wout.at[source, piece],
            send_sem=xsend.at[e, f],
            recv_sem=xrecv.at[e, f],
            device_id={"seq": lax.rem(s + f, seq)},
            device_id_type=MESH,
        )

    stays = (
        pltpu.make_async_copy(
            weight.at[:, pl.ds(pl.multiple_of(a * cols, 128), cols)], wout.at[a], keep.at[0]
        ),
        pltpu.make_async_copy(kw_any.at[:, head], kw, keep.at[1]),
        pltpu.make_async_copy(vw_any.at[:, head], vw, keep.at[2]),
    )
    marks[me] = jnp.broadcast_to(embed_ref[...], (PAD, width))
    for e in range(1, tp):
        mark(e).start()
    for copy in stays:
        copy.start()

    def places(r):
        return ((0, a - r >= 0, a - r), (1, a + r < lines, a + r))

    def along(r, d):
        for way, here, line in places(r):
            slot = line * cross + b

            @pl.when(here)
            def _():
                pass_on(d, slot, way).wait_recv()

            for out in (way, 2, 3):

                @pl.when(jnp.logical_and(here, more[out]))
                def _():
                    pass_on(d, slot, out).start()

    def columns(r):
        return ((2, b - r >= 0, b - r), (3, b + r < cross, b + r))

    def across(d):
        for r in range(1, cross):
            for way, here, col in columns(r):
                for line in range(lines):

                    @pl.when(here)
                    def _():
                        pass_on(d, line * cross + col, way).wait_recv()

                    if cross > 2:

                        @pl.when(jnp.logical_and(here, more[way]))
                        def _():
                            pass_on(d, line * cross + col, way).start()

    def project(part_of):
        rows = part_of(0).shape[0]
        total = jnp.zeros((rows, 1), jnp.float32)
        for t in range(tp):
            part = part_of(t).astype(jnp.float32)
            total = total + jnp.sum(part * part, axis=1, keepdims=True)
        scale = lax.rsqrt(total / (tp * width) + eps)
        q = jnp.zeros((rows, q_cols), jnp.float32)
        k = jnp.zeros((rows, HD), jnp.float32)
        v = jnp.zeros((rows, HD), jnp.float32)
        for t in range(tp):
            here = pl.ds(t * width, width)
            normed = (part_of(t).astype(jnp.float32) * scale * gain_ref[t]).astype(jnp.bfloat16)
            q = q + jnp.dot(normed, qw[here, :], preferred_element_type=jnp.float32)
            k = k + jnp.dot(normed, kw[here, :], preferred_element_type=jnp.float32)
            v = v + jnp.dot(normed, vw[here, :], preferred_element_type=jnp.float32)
        return q + qb[...], k, v + vb[me * KVH // tp]

    last = docs + lines - 2

    def wave(step, carry):
        @pl.when(step + 1 < docs)
        def _():
            held[step + 1, me] = x_ref[step + 1]
            for way in range(4):

                @pl.when(more[way])
                def _():
                    pass_on(step + 1, me, way).start()

        @pl.when(step == 1)
        def _():
            for e in range(1, lines):
                deal(e).start()

        for r in range(1, lines):

            @pl.when(jnp.logical_and(step >= r, step < docs + r))
            def _():
                along(r, step - r)

        @pl.when(step == last)
        def _():
            for e in range(1, tp):
                mark(e).wait_recv()
            stays[1].wait()
            stays[2].wait()
            qm[...], km[...], vm[...] = project(lambda t: marks[t])

        @pl.when(step >= last)
        def _():
            d = step - last
            across(d)
            cosine, sine = cos_ref[...], sin_ref[...]
            q, k, v = project(lambda t: held[d, t])
            q = spin(q, cosine, sine)
            k = spin(k, cosine, sine)
            kv_out[d, s, 0] = k.astype(jnp.bfloat16)
            kv_out[d, s, 1] = v.astype(jnp.bfloat16)
            for e in range(1, seq):
                tell(d, e).start()
            masked = mask_ref[d] == 1
            q_mask = spin(jnp.broadcast_to(qm[0:1, :], (tokens, q_cols)), cosine, sine)
            k_mask = spin(jnp.broadcast_to(km[0:1, :], (tokens, HD)), cosine, sine)
            v_mask = jnp.broadcast_to(vm[0:1, :], (tokens, HD))
            q_out[0, d] = q.astype(jnp.bfloat16)
            q_out[1, d] = jnp.where(masked, q_mask, q).astype(jnp.bfloat16)
            kvn_out[0, d] = jnp.where(masked, k_mask, k).astype(jnp.bfloat16)
            kvn_out[1, d] = jnp.where(masked, v_mask, v).astype(jnp.bfloat16)

        @pl.when(step == lines)
        def _():
            for e in range(1, lines):
                deal(e).wait_recv()
                for f in range(1, seq):
                    share(e, f).start()

        return carry

    lax.fori_loop(-1, last + docs, wave, 0)

    def close(d, carry):
        for e in range(1, seq):
            tell(d, e).wait()
        for r in range(lines):
            for way, here, line in places(r):
                slot = line * cross + b
                outs = (way, way + 2) if r == 0 else (way, 2, 3)
                for out in outs:

                    @pl.when(jnp.logical_and(here, more[out]))
                    def _():
                        pass_on(d, slot, out).wait_send()

        if cross > 2:
            for r in range(1, cross):
                for way, here, col in columns(r):
                    for line in range(lines):

                        @pl.when(jnp.logical_and(here, more[way]))
                        def _():
                            pass_on(d, line * cross + col, way).wait_send()

        return carry

    lax.fori_loop(0, docs, close, 0)
    for e in range(1, tp):
        mark(e).wait_send()
    for e in range(1, lines):
        deal(e).wait_send()
        for f in range(1, seq):
            share(e, f).wait()
    stays[0].wait()


def first(
    clean_in, mask_col, mask_embed, gain, q_weight, q_bias, k_weight, v_weight, v_bias,
    cosine, sine, weight, tp, seq, lines, cross,
):
    docs, tokens, width = clean_in.shape
    d_model, q_cols = q_weight.shape
    vmem = pl.BlockSpec(memory_space=pltpu.VMEM)
    anywhere = pl.BlockSpec(memory_space=pl.ANY)
    dma = pltpu.SemaphoreType.DMA
    bf16 = jnp.bfloat16
    return pl.pallas_call(
        functools.partial(first_kernel, tp, seq, lines, cross),
        out_shape=(
            jax.ShapeDtypeStruct((2, docs, tokens, q_cols), bf16),
            jax.ShapeDtypeStruct((docs, seq, 2, tokens, HD), bf16),
            jax.ShapeDtypeStruct((2, docs, tokens, HD), bf16),
            jax.ShapeDtypeStruct((lines, q_cols, d_model // lines), bf16),
        ),
        in_specs=[vmem] * 6 + [anywhere] * 2 + [vmem] * 3 + [anywhere],
        out_specs=(vmem, vmem, vmem, anywhere),
        scratch_shapes=[
            pltpu.VMEM((docs, tp, tokens, width), bf16),
            pltpu.VMEM((tp, PAD, width), bf16),
            pltpu.VMEM((d_model, HD), bf16),
            pltpu.VMEM((d_model, HD), bf16),
            pltpu.VMEM((PAD, q_cols), jnp.float32),
            pltpu.VMEM((PAD, HD), jnp.float32),
            pltpu.VMEM((PAD, HD), jnp.float32),
            dma((docs, tp, 4)),
            dma((docs, tp)),
            dma((tp,)),
            dma((tp,)),
            dma((docs, seq)),
            dma((docs, seq)),
            dma((lines,)),
            dma((lines,)),
            dma((lines, seq)),
            dma((lines, seq)),
            dma((3,)),
        ],
        compiler_params=pltpu.CompilerParams(
            collective_id=0, has_side_effects=True, vmem_limit_bytes=VMEM_BYTES
        ),
    )(
        clean_in, mask_embed.reshape(1, width), mask_col, gain.reshape(tp, 1, width), q_weight,
        q_bias.reshape(1, -1), k_weight, v_weight, v_bias.reshape(-1, 1, HD), cosine, sine, weight,
    )


def finish_kernel(
    tp, lines, cross, q_ref, kv_ref, kvn_ref, w_ref, x_ref, mask_ref, embed_ref, clean_ref, noisy_ref,
    heads_ref, total_ref, leave_ref, come_ref, send, recv, psend, precv,
):
    greet([("tp", tp)])
    me = lax.axis_index("tp")
    a, b = me // cross, lax.rem(me, cross)
    docs, seq, _, tokens, _ = kv_ref.shape
    q_cols = q_ref.shape[3]
    width = x_ref.shape[2]
    keys = seq * tokens
    scale = 1.0 / math.sqrt(HD)

    def blocks(count, axis, start):
        return (start + lax.broadcasted_iota(jnp.int32, (tokens, count), axis)) // BLOCK

    q_block = blocks(keys, 0, lax.axis_index("seq") * tokens)
    k_block = blocks(keys, 1, 0)
    clean_bias = jnp.where(k_block <= q_block, 0.0, -1e30)
    noisy_bias = jnp.where(k_block < q_block, 0.0, -1e30)
    own_bias = jnp.where(blocks(tokens, 1, 0) == blocks(tokens, 0, 0), 0.0, -1e30)

    def scores(q, k, bias):
        dims = (((1,), (1,)), ((), ()))
        return lax.dot_general(q, k, dims, preferred_element_type=jnp.float32) * scale + bias

    def weigh(expo, v):
        return jnp.dot(expo.astype(jnp.bfloat16), v, preferred_element_type=jnp.float32)

    def pass_on(d, slot, way):
        return pltpu.make_async_remote_copy(
            src_ref=heads_ref.at[d, slot],
            dst_ref=heads_ref.at[d, slot],
            send_sem=send.at[d, slot, way],
            recv_sem=recv.at[d, slot],
            device_id={"tp": lax.rem(me + (cross, tp - cross)[way], tp)},
            device_id_type=MESH,
        )

    more = (a + 1 < lines, a > 0)

    def attend(d):
        k_all = kv_ref[d, :, 0].reshape(keys, HD)
        v_all = kv_ref[d, :, 1].reshape(keys, HD)
        k_own, v_own = kvn_ref[0, d], kvn_ref[1, d]
        for h in range(q_cols // HD):
            cols = pl.ds(h * HD, HD)
            s = scores(q_ref[0, d, :, cols], k_all, clean_bias)
            expo = jnp.exp(s - jnp.max(s, axis=1, keepdims=True))
            denom = jnp.sum(expo, axis=1, keepdims=True)
            heads_ref[d, a, 0, :, cols] = (weigh(expo, v_all) / denom).astype(jnp.bfloat16)
            q = q_ref[1, d, :, cols]
            s = scores(q, k_all, noisy_bias)
            t = scores(q, k_own, own_bias)
            best = jnp.maximum(jnp.max(s, axis=1, keepdims=True), jnp.max(t, axis=1, keepdims=True))
            expo_s, expo_t = jnp.exp(s - best), jnp.exp(t - best)
            denom = jnp.sum(expo_s, axis=1, keepdims=True) + jnp.sum(expo_t, axis=1, keepdims=True)
            total = weigh(expo_s, v_all) + weigh(expo_t, v_own)
            heads_ref[d, a, 1, :, cols] = (total / denom).astype(jnp.bfloat16)
        for way in range(2):

            @pl.when(more[way])
            def _():
                pass_on(d, a, way).start()

    def along(r, d):
        for way, here, slot in ((0, a - r >= 0, a - r), (1, a + r < lines, a + r)):

            @pl.when(here)
            def _():
                pass_on(d, slot, way).wait_recv()

            @pl.when(jnp.logical_and(here, more[way]))
            def _():
                pass_on(d, slot, way).start()

    def partial(d, e):
        return pltpu.make_async_remote_copy(
            src_ref=leave_ref.at[d, e],
            dst_ref=come_ref.at[d, e],
            send_sem=psend.at[d, e],
            recv_sem=precv.at[d, e],
            device_id={"tp": a * cross + lax.rem(b + e, cross)},
            device_id_type=MESH,
        )

    def multiply(d):
        for stream in range(2):
            total = jnp.zeros((tokens, cross * width), jnp.float32)
            for line in range(lines):
                total = total + jnp.dot(
                    heads_ref[d, line, stream], w_ref[line], preferred_element_type=jnp.float32
                )
            for target in range(cross):
                part = total[:, target * width : (target + 1) * width]

                @pl.when(b == target)
                def _():
                    total_ref[d, stream] = part

                @pl.when(b != target)
                def _():
                    leave_ref[d, lax.rem(target - b + cross, cross), stream] = part.astype(
                        jnp.bfloat16
                    )

        for e in range(1, cross):
            partial(d, e).start()

    def wave(step, carry):
        @pl.when(step + 1 < docs)
        def _():
            attend(step + 1)

        for r in range(1, lines):

            @pl.when(jnp.logical_and(step >= r, step < docs + r))
            def _():
                along(r, step - r)

        @pl.when(step >= lines - 1)
        def _():
            multiply(step - (lines - 1))

        return carry

    lax.fori_loop(-1, docs + lines - 1, wave, 0)

    def close(d, carry):
        clean = x_ref[d].astype(jnp.float32)
        noisy = jnp.where(mask_ref[d] == 1, embed_ref[...].astype(jnp.float32), clean)
        for e in range(1, cross):
            partial(d, e).wait_recv()
        for stream, base, out in ((0, clean, clean_ref), (1, noisy, noisy_ref)):
            total = total_ref[d, stream]
            for e in range(1, cross):
                total = total + come_ref[d, e, stream].astype(jnp.float32)
            out[d] = (base + total).astype(jnp.bfloat16)
        for e in range(1, cross):
            partial(d, e).wait_send()
        for r in range(lines):
            for way, here, slot in ((0, a - r >= 0, a - r), (1, a + r < lines, a + r)):

                @pl.when(jnp.logical_and(here, more[way]))
                def _():
                    pass_on(d, slot, way).wait_send()

        return carry

    lax.fori_loop(0, docs, close, 0)


def finish(queries, kv_all, kv_noisy, weight, clean_in, mask_col, mask_embed, tp, lines, cross):
    docs, tokens, width = clean_in.shape
    q_cols = queries.shape[3]
    out = jax.ShapeDtypeStruct(clean_in.shape, jnp.bfloat16)
    vmem = pl.BlockSpec(memory_space=pltpu.VMEM)
    dma = pltpu.SemaphoreType.DMA
    return pl.pallas_call(
        functools.partial(finish_kernel, tp, lines, cross),
        out_shape=(out, out),
        in_specs=[vmem] * 7,
        out_specs=(vmem, vmem),
        scratch_shapes=[
            pltpu.VMEM((docs, lines, 2, tokens, q_cols), jnp.bfloat16),
            pltpu.VMEM((docs, 2, tokens, width), jnp.float32),
            pltpu.VMEM((docs, cross, 2, tokens, width), jnp.bfloat16),
            pltpu.VMEM((docs, cross, 2, tokens, width), jnp.bfloat16),
            dma((docs, lines, 2)),
            dma((docs, lines)),
            dma((docs, cross)),
            dma((docs, cross)),
        ],
        compiler_params=pltpu.CompilerParams(
            collective_id=2, has_side_effects=True, vmem_limit_bytes=VMEM_BYTES
        ),
    )(
        queries,
        kv_all,
        kv_noisy,
        weight,
        clean_in,
        mask_col,
        mask_embed.reshape(1, width),
    )


def per_device(
    tp,
    seq,
    clean_in,
    noise_mask,
    mask_embed,
    norm_gain,
    q_weight,
    q_bias,
    k_weight,
    v_weight,
    v_bias,
    o_weight,
):
    docs, tokens, _ = clean_in.shape
    lines = 4 if tp % 4 == 0 else 1
    cross = tp // lines
    my_seq = lax.axis_index("seq")
    mask_col = noise_mask.reshape(docs, tokens, 1)
    positions = (my_seq * tokens + jnp.arange(tokens)).astype(jnp.float32)
    cosine, sine = tables(positions)
    queries, kv_all, kv_noisy, out_weight = first(
        clean_in, mask_col, mask_embed, norm_gain, q_weight, q_bias, k_weight, v_weight, v_bias,
        cosine, sine, o_weight, tp, seq, lines, cross,
    )
    return finish(
        queries, kv_all, kv_noisy, out_weight, clean_in, mask_col, mask_embed, tp, lines, cross
    )


def solution(mesh):
    return jax.shard_map(
        functools.partial(per_device, mesh.shape["tp"], mesh.shape["seq"]),
        mesh=mesh,
        in_specs=(
            P(None, "seq", "tp"),
            P(None, "seq"),
            P("tp"),
            P(),
            P(None, "tp"),
            P("tp"),
            P(),
            P(),
            P(),
            P("tp", None),
        ),
        out_specs=(P(None, "seq", "tp"), P(None, "seq", "tp")),
        check_vma=False,
    )
```

```python
import functools
import math

import jax
import jax.numpy as jnp
from jax import lax
from jax.experimental import pallas as pl
from jax.experimental.pallas import tpu as pltpu
from jax.sharding import PartitionSpec as P

HD = 128
KVH = 8
BLOCK = 32
PAD = 16

eps = 1e-06
theta = 1000000.0
MESH = pl.DeviceIdType.MESH
VMEM_BYTES = 60 * 2**20


def tables(positions):
    half = HD // 2
    freqs = theta ** (-(jnp.arange(half).astype(jnp.float32) * 2.0) / HD)
    angles = positions[:, None] * freqs[None, :]
    cosine = jnp.cos(angles)
    sine = jnp.sin(angles)
    return jnp.concatenate([cosine, cosine], 1), jnp.concatenate([-sine, sine], 1)


def greet(groups):
    barrier = pltpu.get_barrier_semaphore()
    count = 0
    for axis, size in groups:
        me = lax.axis_index(axis)
        for step in range(1, size):
            pl.semaphore_signal(
                barrier, inc=1, device_id={axis: lax.rem(me + step, size)}, device_id_type=MESH
            )
        count += size - 1
    pl.semaphore_wait(barrier, count)


def spin(values, cosine, sine):
    parts = []
    for start in range(0, values.shape[1], HD):
        head = values[:, start : start + HD]
        parts.append(head * cosine + pltpu.roll(head, HD // 2, 1) * sine)
    return jnp.concatenate(parts, 1) if len(parts) > 1 else parts[0]


def first_kernel(
    tp, seq, lines, cross,
    x_ref, embed_ref, mask_ref, gain_ref, qw, qb, kw_any, vw_any, vb, cos_ref, sin_ref, weight,
    q_out, kv_out, kvn_out, wout,
    held, marks, kvw, qm, km, vm,
    send, recv, msend, mrecv, kvsend, kvrecv, wsend, wrecv, xsend, xrecv, keep,
):
    greet([("tp", tp), ("seq", seq)])
    me = lax.axis_index("tp")
    s = lax.axis_index("seq")
    a, b = me // cross, lax.rem(me, cross)
    docs, tokens, width = x_ref.shape
    q_cols = qw.shape[1]
    head = pl.ds(pl.multiple_of(me * KVH // tp * HD, HD), HD)
    steps = (cross, tp - cross, 1, tp - 1)
    more = (a + 1 < lines, a > 0, b + 1 < cross, b > 0)

    def pass_on(d, slot, way):
        return pltpu.make_async_remote_copy(
            src_ref=held.at[d, slot],
            dst_ref=held.at[d, slot],
            send_sem=send.at[d, slot, way],
            recv_sem=recv.at[d, slot],
            device_id={"tp": lax.rem(me + steps[way], tp)},
            device_id_type=MESH,
        )

    def mark(e):
        return pltpu.make_async_remote_copy(
            src_ref=marks.at[me],
            dst_ref=marks.at[me],
            send_sem=msend.at[e],
            recv_sem=mrecv.at[e],
            device_id={"tp": lax.rem(me + e, tp)},
            device_id_type=MESH,
        )

    def tell(d, e):
        return pltpu.make_async_remote_copy(
            src_ref=kv_out.at[d, s],
            dst_ref=kv_out.at[d, s],
            send_sem=kvsend.at[d, e],
            recv_sem=kvrecv.at[d, e],
            device_id={"seq": lax.rem(s + e, seq)},
            device_id_type=MESH,
        )

    rows = weight.shape[0] // seq
    cols = weight.shape[1] // lines
    piece = pl.ds(pl.multiple_of(s * rows, rows), rows)

    def deal(e):
        to = lax.rem(a + e, lines)
        return pltpu.make_async_remote_copy(
            src_ref=weight.at[piece, pl.ds(pl.multiple_of(to * cols, 128), cols)],
            dst_ref=wout.at[a, piece],
            send_sem=wsend.at[e],
            recv_sem=wrecv.at[e],
            device_id={"tp": to * cross + b},
            device_id_type=MESH,
        )

    def share(e, f):
        source = lax.rem(a + lines - e, lines)
        return pltpu.make_async_remote_copy(
            src_ref=wout.at[source, piece],
            dst_ref=wout.at[source, piece],
            send_sem=xsend.at[e, f],
            recv_sem=xrecv.at[e, f],
            device_id={"seq": lax.rem(s + f, seq)},
            device_id_type=MESH,
        )

    stays = (
        pltpu.make_async_copy(
            weight.at[:, pl.ds(pl.multiple_of(a * cols, 128), cols)], wout.at[a], keep.at[0]
        ),
        pltpu.make_async_copy(kw_any.at[:, head], kvw.at[:, pl.ds(0, HD)], keep.at[1]),
        pltpu.make_async_copy(vw_any.at[:, head], kvw.at[:, pl.ds(HD, HD)], keep.at[2]),
    )
    marks[me] = jnp.broadcast_to(embed_ref[...], (PAD, width))
    for e in range(1, tp):
        mark(e).start()
    for copy in stays:
        copy.start()

    def places(r):
        return ((0, a - r >= 0, a - r), (1, a + r < lines, a + r))

    def along(r, d):
        for way, here, line in places(r):
            slot = line * cross + b

            @pl.when(here)
            def _():
                pass_on(d, slot, way).wait_recv()

            for out in (way, 2, 3):

                @pl.when(jnp.logical_and(here, more[out]))
                def _():
                    pass_on(d, slot, out).start()

    def columns(r):
        return ((2, b - r >= 0, b - r), (3, b + r < cross, b + r))

    def across(d):
        for r in range(1, cross):
            for way, here, col in columns(r):
                for line in range(lines):

                    @pl.when(here)
                    def _():
                        pass_on(d, line * cross + col, way).wait_recv()

                    if cross > 2:

                        @pl.when(jnp.logical_and(here, more[way]))
                        def _():
                            pass_on(d, line * cross + col, way).start()

    def project(part_of):
        rows = part_of(0).shape[0]
        total = jnp.zeros((rows, 1), jnp.float32)
        for t in range(tp):
            part = part_of(t).astype(jnp.float32)
            total = total + jnp.sum(part * part, axis=1, keepdims=True)
        scale = lax.rsqrt(total / (tp * width) + eps)
        q = jnp.zeros((rows, q_cols), jnp.float32)
        kv = jnp.zeros((rows, 2 * HD), jnp.float32)
        for t in range(tp):
            here = pl.ds(t * width, width)
            normed = (part_of(t).astype(jnp.float32) * scale * gain_ref[t]).astype(jnp.bfloat16)
            q = q + jnp.dot(normed, qw[here, :], preferred_element_type=jnp.float32)
            kv = kv + jnp.dot(normed, kvw[here, :], preferred_element_type=jnp.float32)
        return q + qb[...], kv[:, :HD], kv[:, HD:] + vb[me * KVH // tp]

    last = docs + lines - 2

    def wave(step, carry):
        @pl.when(step + 1 < docs)
        def _():
            held[step + 1, me] = x_ref[step + 1]
            for way in range(4):

                @pl.when(more[way])
                def _():
                    pass_on(step + 1, me, way).start()

        @pl.when(step == 1)
        def _():
            for e in range(1, lines):
                deal(e).start()

        for r in range(1, lines):

            @pl.when(jnp.logical_and(step >= r, step < docs + r))
            def _():
                along(r, step - r)

        @pl.when(step == 1)
        def _():
            for e in range(1, tp):
                mark(e).wait_recv()
            stays[1].wait()
            stays[2].wait()
            qm[...], km[...], vm[...] = project(lambda t: marks[t])

        @pl.when(step >= last)
        def _():
            d = step - last
            across(d)
            cosine, sine = cos_ref[...], sin_ref[...]
            q, k, v = project(lambda t: held[d, t])
            q = spin(q, cosine, sine)
            k = spin(k, cosine, sine)
            kv_out[d, s, 0] = k.astype(jnp.bfloat16)
            kv_out[d, s, 1] = v.astype(jnp.bfloat16)
            for e in range(1, seq):
                tell(d, e).start()
            masked = mask_ref[d] == 1
            q_mask = spin(jnp.broadcast_to(qm[0:1, :], (tokens, q_cols)), cosine, sine)
            k_mask = spin(jnp.broadcast_to(km[0:1, :], (tokens, HD)), cosine, sine)
            v_mask = jnp.broadcast_to(vm[0:1, :], (tokens, HD))
            q_out[0, d] = q.astype(jnp.bfloat16)
            q_out[1, d] = jnp.where(masked, q_mask, q).astype(jnp.bfloat16)
            kvn_out[0, d] = jnp.where(masked, k_mask, k).astype(jnp.bfloat16)
            kvn_out[1, d] = jnp.where(masked, v_mask, v).astype(jnp.bfloat16)

        @pl.when(step == lines)
        def _():
            for e in range(1, lines):
                deal(e).wait_recv()
                for f in range(1, seq):
                    share(e, f).start()

        return carry

    lax.fori_loop(-1, last + docs, wave, 0)

    def close(d, carry):
        for e in range(1, seq):
            tell(d, e).wait()
        for r in range(lines):
            for way, here, line in places(r):
                slot = line * cross + b
                outs = (way, way + 2) if r == 0 else (way, 2, 3)
                for out in outs:

                    @pl.when(jnp.logical_and(here, more[out]))
                    def _():
                        pass_on(d, slot, out).wait_send()

        if cross > 2:
            for r in range(1, cross):
                for way, here, col in columns(r):
                    for line in range(lines):

                        @pl.when(jnp.logical_and(here, more[way]))
                        def _():
                            pass_on(d, line * cross + col, way).wait_send()

        return carry

    lax.fori_loop(0, docs, close, 0)
    for e in range(1, tp):
        mark(e).wait_send()
    for e in range(1, lines):
        deal(e).wait_send()
        for f in range(1, seq):
            share(e, f).wait()
    stays[0].wait()


def first(
    clean_in, mask_col, mask_embed, gain, q_weight, q_bias, k_weight, v_weight, v_bias,
    cosine, sine, weight, tp, seq, lines, cross,
):
    docs, tokens, width = clean_in.shape
    d_model, q_cols = q_weight.shape
    vmem = pl.BlockSpec(memory_space=pltpu.VMEM)
    anywhere = pl.BlockSpec(memory_space=pl.ANY)
    dma = pltpu.SemaphoreType.DMA
    bf16 = jnp.bfloat16
    return pl.pallas_call(
        functools.partial(first_kernel, tp, seq, lines, cross),
        out_shape=(
            jax.ShapeDtypeStruct((2, docs, tokens, q_cols), bf16),
            jax.ShapeDtypeStruct((docs, seq, 2, tokens, HD), bf16),
            jax.ShapeDtypeStruct((2, docs, tokens, HD), bf16),
            jax.ShapeDtypeStruct((lines, q_cols, d_model // lines), bf16),
        ),
        in_specs=[vmem] * 6 + [anywhere] * 2 + [vmem] * 3 + [anywhere],
        out_specs=(vmem, vmem, vmem, anywhere),
        scratch_shapes=[
            pltpu.VMEM((docs, tp, tokens, width), bf16),
            pltpu.VMEM((tp, PAD, width), bf16),
            pltpu.VMEM((d_model, 2 * HD), bf16),
            pltpu.VMEM((PAD, q_cols), jnp.float32),
            pltpu.VMEM((PAD, HD), jnp.float32),
            pltpu.VMEM((PAD, HD), jnp.float32),
            dma((docs, tp, 4)),
            dma((docs, tp)),
            dma((tp,)),
            dma((tp,)),
            dma((docs, seq)),
            dma((docs, seq)),
            dma((lines,)),
            dma((lines,)),
            dma((lines, seq)),
            dma((lines, seq)),
            dma((3,)),
        ],
        compiler_params=pltpu.CompilerParams(
            collective_id=0, has_side_effects=True, vmem_limit_bytes=VMEM_BYTES
        ),
    )(
        clean_in, mask_embed.reshape(1, width), mask_col, gain.reshape(tp, 1, width), q_weight,
        q_bias.reshape(1, -1), k_weight, v_weight, v_bias.reshape(-1, 1, HD), cosine, sine, weight,
    )


def finish_kernel(
    tp, lines, cross, q_ref, kv_ref, kvn_ref, w_ref, x_ref, mask_ref, embed_ref, clean_ref, noisy_ref,
    heads_ref, total_ref, leave_ref, come_ref, send, recv, psend, precv,
):
    greet([("tp", tp)])
    me = lax.axis_index("tp")
    a, b = me // cross, lax.rem(me, cross)
    docs, seq, _, tokens, _ = kv_ref.shape
    q_cols = q_ref.shape[3]
    width = x_ref.shape[2]
    keys = seq * tokens
    scale = 1.0 / math.sqrt(HD)

    def blocks(count, axis, start):
        return (start + lax.broadcasted_iota(jnp.int32, (tokens, count), axis)) // BLOCK

    q_block = blocks(keys, 0, lax.axis_index("seq") * tokens)
    k_block = blocks(keys, 1, 0)
    clean_bias = jnp.where(k_block <= q_block, 0.0, -1e30)
    noisy_bias = jnp.where(k_block < q_block, 0.0, -1e30)
    own_bias = jnp.where(blocks(tokens, 1, 0) == blocks(tokens, 0, 0), 0.0, -1e30)

    def scores(q, k, bias):
        dims = (((1,), (1,)), ((), ()))
        return lax.dot_general(q, k, dims, preferred_element_type=jnp.float32) * scale + bias

    def weigh(expo, v):
        return jnp.dot(expo.astype(jnp.bfloat16), v, preferred_element_type=jnp.float32)

    def pass_on(d, slot, way):
        return pltpu.make_async_remote_copy(
            src_ref=heads_ref.at[d, slot],
            dst_ref=heads_ref.at[d, slot],
            send_sem=send.at[d, slot, way],
            recv_sem=recv.at[d, slot],
            device_id={"tp": lax.rem(me + (cross, tp - cross)[way], tp)},
            device_id_type=MESH,
        )

    more = (a + 1 < lines, a > 0)

    def attend(d):
        k_all = kv_ref[d, :, 0].reshape(keys, HD)
        v_all = kv_ref[d, :, 1].reshape(keys, HD)
        k_own, v_own = kvn_ref[0, d], kvn_ref[1, d]
        for h in range(q_cols // HD):
            cols = pl.ds(h * HD, HD)
            s = scores(q_ref[0, d, :, cols], k_all, clean_bias)
            expo = jnp.exp(s - jnp.max(s, axis=1, keepdims=True))
            denom = jnp.sum(expo, axis=1, keepdims=True)
            heads_ref[d, a, 0, :, cols] = (weigh(expo, v_all) / denom).astype(jnp.bfloat16)
            q = q_ref[1, d, :, cols]
            s = scores(q, k_all, noisy_bias)
            t = scores(q, k_own, own_bias)
            best = jnp.maximum(jnp.max(s, axis=1, keepdims=True), jnp.max(t, axis=1, keepdims=True))
            expo_s, expo_t = jnp.exp(s - best), jnp.exp(t - best)
            denom = jnp.sum(expo_s, axis=1, keepdims=True) + jnp.sum(expo_t, axis=1, keepdims=True)
            total = weigh(expo_s, v_all) + weigh(expo_t, v_own)
            heads_ref[d, a, 1, :, cols] = (total / denom).astype(jnp.bfloat16)
        for way in range(2):

            @pl.when(more[way])
            def _():
                pass_on(d, a, way).start()

    def along(r, d):
        for way, here, slot in ((0, a - r >= 0, a - r), (1, a + r < lines, a + r)):

            @pl.when(here)
            def _():
                pass_on(d, slot, way).wait_recv()

            @pl.when(jnp.logical_and(here, more[way]))
            def _():
                pass_on(d, slot, way).start()

    def partial(d, e):
        return pltpu.make_async_remote_copy(
            src_ref=leave_ref.at[d, e],
            dst_ref=come_ref.at[d, e],
            send_sem=psend.at[d, e],
            recv_sem=precv.at[d, e],
            device_id={"tp": a * cross + lax.rem(b + e, cross)},
            device_id_type=MESH,
        )

    def multiply(d):
        for stream in range(2):
            total = jnp.zeros((tokens, cross * width), jnp.float32)
            for line in range(lines):
                total = total + jnp.dot(
                    heads_ref[d, line, stream], w_ref[line], preferred_element_type=jnp.float32
                )
            for target in range(cross):
                part = total[:, target * width : (target + 1) * width]

                @pl.when(b == target)
                def _():
                    total_ref[d, stream] = part

                @pl.when(b != target)
                def _():
                    leave_ref[d, lax.rem(target - b + cross, cross), stream] = part.astype(
                        jnp.bfloat16
                    )

        for e in range(1, cross):
            partial(d, e).start()

    def wave(step, carry):
        @pl.when(step + 1 < docs)
        def _():
            attend(step + 1)

        for r in range(1, lines):

            @pl.when(jnp.logical_and(step >= r, step < docs + r))
            def _():
                along(r, step - r)

        @pl.when(step >= lines - 1)
        def _():
            multiply(step - (lines - 1))

        return carry

    lax.fori_loop(-1, docs + lines - 1, wave, 0)

    def close(d, carry):
        clean = x_ref[d].astype(jnp.float32)
        noisy = jnp.where(mask_ref[d] == 1, embed_ref[...].astype(jnp.float32), clean)
        for e in range(1, cross):
            partial(d, e).wait_recv()
        for stream, base, out in ((0, clean, clean_ref), (1, noisy, noisy_ref)):
            total = total_ref[d, stream]
            for e in range(1, cross):
                total = total + come_ref[d, e, stream].astype(jnp.float32)
            out[d] = (base + total).astype(jnp.bfloat16)
        for e in range(1, cross):
            partial(d, e).wait_send()
        for r in range(lines):
            for way, here, slot in ((0, a - r >= 0, a - r), (1, a + r < lines, a + r)):

                @pl.when(jnp.logical_and(here, more[way]))
                def _():
                    pass_on(d, slot, way).wait_send()

        return carry

    lax.fori_loop(0, docs, close, 0)


def finish(queries, kv_all, kv_noisy, weight, clean_in, mask_col, mask_embed, tp, lines, cross):
    docs, tokens, width = clean_in.shape
    q_cols = queries.shape[3]
    out = jax.ShapeDtypeStruct(clean_in.shape, jnp.bfloat16)
    vmem = pl.BlockSpec(memory_space=pltpu.VMEM)
    dma = pltpu.SemaphoreType.DMA
    return pl.pallas_call(
        functools.partial(finish_kernel, tp, lines, cross),
        out_shape=(out, out),
        in_specs=[vmem] * 7,
        out_specs=(vmem, vmem),
        scratch_shapes=[
            pltpu.VMEM((docs, lines, 2, tokens, q_cols), jnp.bfloat16),
            pltpu.VMEM((docs, 2, tokens, width), jnp.float32),
            pltpu.VMEM((docs, cross, 2, tokens, width), jnp.bfloat16),
            pltpu.VMEM((docs, cross, 2, tokens, width), jnp.bfloat16),
            dma((docs, lines, 2)),
            dma((docs, lines)),
            dma((docs, cross)),
            dma((docs, cross)),
        ],
        compiler_params=pltpu.CompilerParams(
            collective_id=2, has_side_effects=True, vmem_limit_bytes=VMEM_BYTES
        ),
    )(
        queries,
        kv_all,
        kv_noisy,
        weight,
        clean_in,
        mask_col,
        mask_embed.reshape(1, width),
    )


def per_device(
    tp,
    seq,
    clean_in,
    noise_mask,
    mask_embed,
    norm_gain,
    q_weight,
    q_bias,
    k_weight,
    v_weight,
    v_bias,
    o_weight,
):
    docs, tokens, _ = clean_in.shape
    lines = 4 if tp % 4 == 0 else 1
    cross = tp // lines
    my_seq = lax.axis_index("seq")
    mask_col = noise_mask.reshape(docs, tokens, 1)
    positions = (my_seq * tokens + jnp.arange(tokens)).astype(jnp.float32)
    cosine, sine = tables(positions)
    queries, kv_all, kv_noisy, out_weight = first(
        clean_in, mask_col, mask_embed, norm_gain, q_weight, q_bias, k_weight, v_weight, v_bias,
        cosine, sine, o_weight, tp, seq, lines, cross,
    )
    return finish(
        queries, kv_all, kv_noisy, out_weight, clean_in, mask_col, mask_embed, tp, lines, cross
    )


def solution(mesh):
    return jax.shard_map(
        functools.partial(per_device, mesh.shape["tp"], mesh.shape["seq"]),
        mesh=mesh,
        in_specs=(
            P(None, "seq", "tp"),
            P(None, "seq"),
            P("tp"),
            P(),
            P(None, "tp"),
            P("tp"),
            P(),
            P(),
            P(),
            P("tp", None),
        ),
        out_specs=(P(None, "seq", "tp"), P(None, "seq", "tp")),
        check_vma=False,
    )
```
